32 devices in a mesh: fsdp: 4 (over x, core), tp: 8 (over z, y).
Axes of the slice: x: 2, y: 2, z: 4, core: 2. Of those that a mesh axis runs over, the one named last changes fastest.
Arguments:
- inputs: bfloat16 [128, 4, 8192], P('tp', None, 'fsdp'), may hold values from -6 to 6
- featurizer: bfloat16 [8192, 3, 8192], P('fsdp', None, 'tp'), may hold values from -0.0625 to 0.0625
- short_filter: float32 [3, 3, 8192], P(None, None, 'tp'), may hold values from -3 to 3
- long_filter: float32 [512, 128], P('tp'), may hold values from -1.2 to 1.2
- decay_rate: float32 [512], P('tp'), may hold values from 0.004 to 0.08
- skip_gain: float32 [8192], P('tp'), may hold values from -1 to 1
- output_grad: bfloat16 [128, 4, 8192], P(None, 'fsdp', 'tp'), may hold values from -6 to 6
Outputs:
- hyena_out: bfloat16 [128, 4, 8192], P(None, 'fsdp', 'tp')
- input_grad: bfloat16 [128, 4, 8192], P('tp', None, 'fsdp')
- weight_grad: bfloat16 [8192, 3, 8192], P('fsdp', None, 'tp')
The draws below stay inside these ranges and needn't reach their ends.
All inputs are finite; a program needn't handle non-finite values.
Results may differ from the reference program's by a relative error of at most 0.028.
Values may be sent and summed in bfloat16 or wider, within the bound.
A program may use at most 128 MiB of HBM per device.

```python
import math
import jax
import jax.numpy as jnp
from jax import lax

D = 8192
HC = 8192
CH_GROUP = 16
FILT_LEN = 128
SHORT_LEN = 3
TOK = 128
BLOCKS = 4
SEQ_LEN = 512
FILTERS = 512
N_TP = 8


def level_of(key, shape, split, smallest, high):
    def one(axis_at, shards_of):
        steps = jax.random.uniform(jax.random.fold_in(jax.random.fold_in(key, 6), axis_at), (shards_of,), jnp.float32, smallest / len(split), high / len(split))
        return jnp.repeat(jnp.exp(steps), shape[axis_at] // shards_of).reshape((-1,) + (1,) * (len(shape) - axis_at - 1))

    gain = one(*split[0])
    for cut in split[1:]:
        gain = gain * one(*cut)
    return gain


def bell_draw(own_key, extent, scale, limit, pieces=(), kind=jnp.bfloat16):
    entries = jax.random.normal(own_key, extent, jnp.float32) * scale
    if len(pieces) > 0:
        entries = level_of(own_key, extent, pieces, -0.22, 0.18) * entries
    return jnp.clip(entries, min=-limit, max=limit).astype(kind)


def setup_inputs(seed: int = 0) -> dict:
    arg_keys = jax.random.split(jax.random.key(seed), 8)
    return {
        "inputs": bell_draw(arg_keys[0], (TOK, BLOCKS, D), 1.0, 6.0, ((0, 8), (2, 4))),
        "featurizer": bell_draw(arg_keys[1], (D, 3, HC), D ** -0.5, 0.0625, ((0, 4), (2, 8))),
        "short_filter": bell_draw(arg_keys[2], (SHORT_LEN, 3, HC), 0.6, 3.0, ((2, 8),), jnp.float32),
        "long_filter": bell_draw(arg_keys[3], (FILTERS, FILT_LEN), 0.2, 1.2, ((0, 8),), jnp.float32),
        "decay_rate": jnp.clip(jnp.exp(math.log(0.08) - 2.9957322 * jax.random.uniform(arg_keys[4], (FILTERS,), jnp.float32) ** level_of(arg_keys[4], (FILTERS,), ((0, 8),), -0.2, 0.2)), 0.004, 0.08),
        "skip_gain": jnp.clip(jax.random.uniform(arg_keys[5], (HC,), jnp.float32, -1.0, 1.0) * level_of(arg_keys[5], (HC,), ((0, 8),), -0.4, 0.0), -1.0, 1.0),
        "output_grad": bell_draw(arg_keys[6], (TOK, BLOCKS, HC), 1.0, 6.0, ((1, 4), (2, 8))),
    }


def delayed(values, steps):
    if steps == 0:
        return values
    padding = jnp.zeros((steps,) + values.shape[1:], values.dtype)
    return jnp.concatenate([padding, values[:values.shape[0] - steps]], 0)


def advanced(values, steps):
    if steps == 0:
        return values
    padding = jnp.zeros((steps,) + values.shape[1:], values.dtype)
    return jnp.concatenate([values[steps:], padding], 0)


def toeplitz_pair(kernel, tokens):
    tap_count = kernel.shape[1]
    positions = jnp.arange(tokens).astype(jnp.int32)
    lag_grid = positions[:, None] - positions[None, :]
    near_inside = (lag_grid >= 0) & (lag_grid < tap_count)
    near_taken = jnp.take(kernel, jnp.clip(lag_grid, 0, tap_count - 1).astype(jnp.int32), axis=1)
    near_matrix = jnp.where(near_inside[None], near_taken, jnp.zeros_like(near_taken))
    far_grid = lag_grid + tokens
    far_inside = far_grid < tap_count
    far_taken = jnp.take(kernel, jnp.clip(far_grid, 0, tap_count - 1).astype(jnp.int32), axis=1)
    far_matrix = jnp.where(far_inside[None], far_taken, jnp.zeros_like(far_taken))
    return near_matrix, far_matrix


def hyena_layer(features, short_filter, long_filter, decay_rate, skip_gain, output_grad):
    feat_wide = features.astype(jnp.float32)
    filtered = short_filter[0] * feat_wide
    for lag_step in range(1, SHORT_LEN):
        filtered = filtered + short_filter[lag_step] * delayed(feat_wide, lag_step)
    queries = filtered[:, 0]
    key_part = filtered[:, 1]
    value_part = filtered[:, 2]
    product = key_part * value_part
    offsets = jnp.arange(FILT_LEN).astype(jnp.float32)
    kernel = long_filter * jnp.exp(-decay_rate[:, None] * offsets[None, :])
    near_matrix, far_matrix = toeplitz_pair(kernel, TOK)
    grouped = product.reshape(BLOCKS, TOK, FILTERS, CH_GROUP)
    earlier = delayed(grouped, 1)
    convolved = jnp.einsum("nst,btnc->bsnc", near_matrix, grouped, precision=lax.Precision.HIGHEST)
    convolved = convolved + jnp.einsum("nst,btnc->bsnc", far_matrix, earlier, precision=lax.Precision.HIGHEST)
    convolved = convolved.reshape(SEQ_LEN, HC) + skip_gain * product
    output = (queries * convolved).astype(jnp.bfloat16)
    upstream = output_grad.astype(jnp.float32)
    query_grad = upstream * convolved
    conv_grad = upstream * queries
    conv_grouped = conv_grad.reshape(BLOCKS, TOK, FILTERS, CH_GROUP)
    later_grad = advanced(conv_grouped, 1)
    product_grad = jnp.einsum("nst,bsnc->btnc", near_matrix, conv_grouped, precision=lax.Precision.HIGHEST)
    product_grad = product_grad + jnp.einsum("nst,bsnc->btnc", far_matrix, later_grad, precision=lax.Precision.HIGHEST)
    product_grad = product_grad.reshape(SEQ_LEN, HC) + skip_gain * conv_grad
    filtered_grad = jnp.stack([query_grad, product_grad * value_part, product_grad * key_part], axis=1)
    feature_grad = short_filter[0] * filtered_grad
    for lag_step in range(1, SHORT_LEN):
        feature_grad = feature_grad + short_filter[lag_step] * advanced(filtered_grad, lag_step)
    return output, feature_grad.astype(jnp.bfloat16)


def reference(inputs, featurizer, short_filter, long_filter, decay_rate, skip_gain, output_grad):
    flat_inputs = inputs.reshape(TOK * BLOCKS, D)
    features = jnp.dot(flat_inputs, featurizer.reshape(D, 3 * HC), preferred_element_type=jnp.float32)
    features = features.astype(jnp.bfloat16).reshape(TOK, BLOCKS, 3, HC)
    seq_features = features.transpose(1, 0, 2, 3).reshape(SEQ_LEN, 3, HC)
    seq_grad = output_grad.transpose(1, 0, 2).reshape(SEQ_LEN, HC)
    seq_output, seq_feature_grad = hyena_layer(seq_features, short_filter, long_filter, decay_rate, skip_gain, seq_grad)
    hyena_out = seq_output.reshape(BLOCKS, TOK, HC).transpose(1, 0, 2)
    feature_grad = seq_feature_grad.reshape(BLOCKS, TOK, 3, HC).transpose(1, 0, 2, 3)
    weight_grad = lax.dot_general(inputs, feature_grad, (((0, 1), (0, 1)), ((), ())), preferred_element_type=jnp.float32)
    weight_grad = weight_grad.astype(jnp.bfloat16)
    slab_width = HC // N_TP
    grad_blocks = feature_grad.reshape(TOK * BLOCKS, 3, N_TP, slab_width).transpose(2, 0, 1, 3).reshape(N_TP, TOK * BLOCKS, 3 * slab_width)
    weight_blocks = featurizer.reshape(D, 3, N_TP, slab_width).transpose(2, 0, 1, 3).reshape(N_TP, D, 3 * slab_width)

    def add_slab(running, operands):
        partial_value = lax.dot_general(operands[0], operands[1], (((1,), (1,)), ((), ())), preferred_element_type=jnp.float32)
        rounded = lax.optimization_barrier(partial_value.astype(jnp.bfloat16))
        return running + rounded.astype(jnp.float32), None

    running, unused = lax.scan(add_slab, jnp.zeros((TOK * BLOCKS, D), jnp.float32), (grad_blocks, weight_blocks))
    input_grad = running.astype(jnp.bfloat16).reshape(TOK, BLOCKS, D)
    return hyena_out, input_grad, weight_grad
```

```python
import functools

import jax
import jax.numpy as jnp
from jax import lax
from jax.experimental import pallas as pl
from jax.experimental.pallas import tpu as pltpu
from jax.sharding import PartitionSpec as P

F32 = jnp.float32
BF16 = jnp.bfloat16
MESH = pl.DeviceIdType.MESH
VMEM = pl.BlockSpec(memory_space=pltpu.VMEM)
LANES = 128
HALO = 16
HEAD = 8


def hyena_kernel(
    blocks, width, feat, short, taps, taps_back, skip, upstream, out, grad,
    ext_p, ext_g, query, key, value, prod, conv_grad, filt_grad, sems, head_sems,
):
    me = lax.axis_index("fsdp")
    rest = lax.axis_index("tp")
    tokens, channels = out.shape
    taps_count = taps.shape[1]
    has_prev = me > 0
    has_next = me < blocks - 1
    prev = jnp.maximum(me - 1, 0)
    later = jnp.minimum(me + 1, blocks - 1)
    barrier = pltpu.get_barrier_semaphore()

    for peer in (lax.rem(me + 1, blocks), lax.rem(me + blocks - 1, blocks)):
        pl.semaphore_signal(barrier, inc=1, device_id=(peer, rest), device_id_type=MESH)
    pl.semaphore_wait(barrier, 2)

    def front(at, _):
        cols = pl.ds(pl.multiple_of(at * LANES, LANES), LANES)
        parts = []
        for i in range(3):
            f = feat[i, :, cols].astype(F32)
            acc = short[pl.ds(i, 1), cols] * f[HALO:]
            for j in range(1, 3):
                acc = acc + short[pl.ds(3 * j + i, 1), cols] * pltpu.roll(f, j, 0)[HALO:]
            parts.append(acc)
        p = parts[1] * parts[2]
        cg = upstream[:, cols].astype(F32) * parts[0]
        query[:, cols] = parts[0]
        key[:, cols] = parts[1]
        value[:, cols] = parts[2]
        prod[:, cols] = p
        conv_grad[:, cols] = cg
        ext_p[pl.ds(tokens, tokens), cols] = p.astype(BF16)
        ext_g[pl.ds(0, tokens), cols] = cg.astype(BF16)
        return 0

    lax.fori_loop(0, channels // LANES, front, 0)

    to_next = pltpu.make_async_remote_copy(
        src_ref=ext_p.at[pl.ds(tokens, tokens)], dst_ref=ext_p.at[pl.ds(0, tokens)],
        send_sem=sems.at[0], recv_sem=sems.at[1], device_id=(later, rest), device_id_type=MESH)
    to_prev = pltpu.make_async_remote_copy(
        src_ref=ext_g.at[pl.ds(0, tokens)], dst_ref=ext_g.at[pl.ds(tokens, tokens)],
        send_sem=sems.at[2], recv_sem=sems.at[3], device_id=(prev, rest), device_id_type=MESH)

    @pl.when(has_next)
    def _():
        to_next.start()

    @pl.when(has_prev)
    def _():
        to_prev.start()

    @pl.when(jnp.logical_not(has_prev))
    def _():
        ext_p[pl.ds(0, tokens), :] = jnp.zeros((tokens, channels), BF16)

    @pl.when(jnp.logical_not(has_next))
    def _():
        ext_g[pl.ds(tokens, tokens), :] = jnp.zeros((tokens, channels), BF16)

    @pl.when(has_prev)
    def _():
        to_next.wait_recv()

    @pl.when(has_next)
    def _():
        to_prev.wait_recv()

    per_tile = LANES // width
    lane = lax.broadcasted_iota(jnp.int32, (tokens, LANES), 1) // width

    def mixed(rows, ext, first):
        acc = None
        for g in range(per_tile):
            line = jnp.concatenate([rows[g : g + 1], jnp.zeros((1, 2 * tokens - taps_count), F32)], axis=1)
            wide = jnp.broadcast_to(line, (tokens, 2 * tokens))
            toeplitz = pltpu.roll(wide, first, 1, stride=1, stride_axis=0).astype(BF16)
            part = jnp.dot(toeplitz, ext, preferred_element_type=F32)
            acc = part if acc is None else jnp.where(lane == g, part, acc)
        return acc

    def back(at, _):
        cols = pl.ds(pl.multiple_of(at * LANES, LANES), LANES)
        rows = pl.ds(pl.multiple_of(at * per_tile, per_tile), per_tile)
        gain = skip[:, cols]
        conv = mixed(taps_back[rows, :], ext_p[:, cols], 1 + tokens - taps_count) + gain * prod[:, cols]
        pg = mixed(taps[rows, :], ext_g[:, cols], 0) + gain * conv_grad[:, cols]
        out[:, cols] = (query[:, cols] * conv).astype(BF16)
        own = pl.ds(0, tokens)
        filt_grad[0, own, cols] = upstream[:, cols].astype(F32) * conv
        filt_grad[1, own, cols] = pg * value[:, cols]
        filt_grad[2, own, cols] = pg * key[:, cols]
        return 0

    lax.fori_loop(0, channels // LANES, back, 0)

    head = pltpu.make_async_remote_copy(
        src_ref=filt_grad.at[:, pl.ds(0, HEAD)], dst_ref=filt_grad.at[:, pl.ds(tokens, HEAD)],
        send_sem=head_sems.at[0], recv_sem=head_sems.at[1], device_id=(prev, rest), device_id_type=MESH)

    @pl.when(has_prev)
    def _():
        head.start()

    @pl.when(jnp.logical_not(has_next))
    def _():
        filt_grad[:, pl.ds(tokens, HEAD), :] = jnp.zeros((3, HEAD, channels), F32)

    @pl.when(has_next)
    def _():
        head.wait_recv()

    def last(at, _):
        cols = pl.ds(pl.multiple_of(at * LANES, LANES), LANES)
        for i in range(3):
            f = filt_grad[i, :, cols]
            acc = short[pl.ds(i, 1), cols] * f[:tokens]
            for j in range(1, 3):
                acc = acc + short[pl.ds(3 * j + i, 1), cols] * pltpu.roll(f, tokens + HEAD - j, 0)[:tokens]
            grad[i, :, cols] = acc.astype(BF16)
        return 0

    lax.fori_loop(0, channels // LANES, last, 0)

    @pl.when(has_next)
    def _():
        to_next.wait_send()

    @pl.when(has_prev)
    def _():
        to_prev.wait_send()
        head.wait_send()


def hyena(feat, short_filter, long_filter, decay_rate, skip_gain, upstream):
    tokens, channels = upstream.shape
    taps = long_filter * jnp.exp(-decay_rate[:, None] * jnp.arange(long_filter.shape[1]).astype(F32)[None, :])
    width = channels // long_filter.shape[0]
    wide = pltpu.VMEM((tokens, channels), F32)
    return pl.pallas_call(
        functools.partial(hyena_kernel, lax.axis_size("fsdp"), width),
        out_shape=(jax.ShapeDtypeStruct((tokens, channels), BF16), jax.ShapeDtypeStruct((3, tokens, channels), BF16)),
        in_specs=[VMEM] * 6,
        out_specs=(VMEM, VMEM),
        scratch_shapes=[
            pltpu.VMEM((2 * tokens, channels), BF16), pltpu.VMEM((2 * tokens, channels), BF16),
            wide, wide, wide, wide, wide, pltpu.VMEM((3, tokens + HEAD, channels), F32),
            pltpu.SemaphoreType.DMA((4,)), pltpu.SemaphoreType.DMA((2,)),
        ],
        compiler_params=pltpu.CompilerParams(collective_id=1, has_side_effects=True, vmem_limit_bytes=40 * 2**20),
    )(feat, short_filter.reshape(9, channels), taps, taps[:, ::-1], skip_gain[None], upstream)


def weight_kernel(x, g, out):
    out[...] = lax.dot_general(x[...], g[...], (((0,), (0,)), ((), ())), preferred_element_type=F32).astype(BF16)


def weight_product(x, grads):
    rows, depth = x.shape
    channels = grads.shape[2]
    step = min(512, depth)
    return pl.pallas_call(
        weight_kernel,
        grid=(depth // step, 3),
        out_shape=jax.ShapeDtypeStruct((3, depth, channels), BF16),
        in_specs=[
            pl.BlockSpec((rows, step), lambda d, i: (0, d)),
            pl.BlockSpec((None, rows, channels), lambda d, i: (i, 0, 0)),
        ],
        out_specs=pl.BlockSpec((None, step, channels), lambda d, i: (i, d, 0)),
        compiler_params=pltpu.CompilerParams(vmem_limit_bytes=40 * 2**20),
        cost_estimate=pl.CostEstimate(
            flops=6 * rows * depth * channels, bytes_accessed=2 * 3 * depth * channels, transcendentals=0),
    )(x, grads)


def shards(inputs, featurizer, short_filter, long_filter, decay_rate, skip_gain, output_grad):
    weights = featurizer.transpose(1, 0, 2)
    gathered = lax.all_gather(inputs.transpose(1, 0, 2), "tp", axis=1, tiled=True)
    blocks, tokens, depth = gathered.shape
    channels = weights.shape[2]
    border = jnp.zeros((1, HALO, depth), BF16)
    earlier = jnp.concatenate([border, gathered[: blocks - 1, tokens - HALO :]], axis=0)
    extended = jnp.concatenate([earlier, gathered], axis=1).reshape(blocks * (tokens + HALO), depth)
    feats = []
    for i in range(3):
        part = jnp.dot(extended, weights[i], preferred_element_type=F32).astype(BF16)
        part = part.reshape(blocks, tokens + HALO, channels)
        swapped = lax.all_to_all(part, "fsdp", split_axis=0, concat_axis=0, tiled=True)
        feats.append(jnp.sum(swapped.astype(F32), axis=0).astype(BF16))
    out, own_grad = hyena(
        jnp.stack(feats), short_filter, long_filter, decay_rate, skip_gain, output_grad.reshape(tokens, channels))
    grads = lax.all_gather(own_grad, "fsdp", axis=1, tiled=True)
    turned = grads.reshape(3, blocks, tokens, channels).transpose(0, 2, 1, 3).reshape(grads.shape)
    part = None
    for i in range(3):
        term = lax.dot_general(turned[i], weights[i], (((1,), (1,)), ((), ())), preferred_element_type=F32)
        part = term if part is None else part + term
    weight_grad = weight_product(gathered.reshape(blocks * tokens, depth), grads)
    input_grad = lax.psum_scatter(
        part.astype(BF16).reshape(tokens, blocks, depth), "tp", scatter_dimension=0, tiled=True)
    return out.reshape(output_grad.shape), input_grad, weight_grad.transpose(1, 0, 2)


def solution(mesh):
    in_specs = (
        P("tp", None, "fsdp"),
        P("fsdp", None, "tp"),
        P(None, None, "tp"),
        P("tp", None),
        P("tp"),
        P("tp"),
        P(None, "fsdp", "tp"),
    )
    out_specs = (P(None, "fsdp", "tp"), P("tp", None, "fsdp"), P("fsdp", None, "tp"))
    return jax.shard_map(shards, mesh=mesh, in_specs=in_specs, out_specs=out_specs, check_vma=False)
```

```python
import functools

import jax
import jax.numpy as jnp
from jax import lax
from jax.experimental import pallas as pl
from jax.experimental.pallas import tpu as pltpu
from jax.sharding import PartitionSpec as P

F32 = jnp.float32
BF16 = jnp.bfloat16
MESH = pl.DeviceIdType.MESH
VMEM = pl.BlockSpec(memory_space=pltpu.VMEM)
LANES = 128
HALO = 16
HEAD = 8


def hyena_kernel(
    blocks, width, feat, short, taps, taps_back, skip, upstream, out, grad,
    ext_p, ext_g, query, key, value, prod, conv_grad, filt_grad, sems, head_sems,
):
    me = lax.axis_index("fsdp")
    rest = lax.axis_index("tp")
    tokens, channels = out.shape
    taps_count = taps.shape[1]
    has_prev = me > 0
    has_next = me < blocks - 1
    prev = jnp.maximum(me - 1, 0)
    later = jnp.minimum(me + 1, blocks - 1)
    barrier = pltpu.get_barrier_semaphore()

    for peer in (lax.rem(me + 1, blocks), lax.rem(me + blocks - 1, blocks)):
        pl.semaphore_signal(barrier, inc=1, device_id=(peer, rest), device_id_type=MESH)
    pl.semaphore_wait(barrier, 2)

    def front(at, _):
        cols = pl.ds(pl.multiple_of(at * LANES, LANES), LANES)
        parts = []
        for i in range(3):
            f = feat[i, :, cols].astype(F32)
            acc = short[pl.ds(i, 1), cols] * f[HALO:]
            for j in range(1, 3):
                acc = acc + short[pl.ds(3 * j + i, 1), cols] * pltpu.roll(f, j, 0)[HALO:]
            parts.append(acc)
        p = parts[1] * parts[2]
        cg = upstream[:, cols].astype(F32) * parts[0]
        query[:, cols] = parts[0]
        key[:, cols] = parts[1]
        value[:, cols] = parts[2]
        prod[:, cols] = p
        conv_grad[:, cols] = cg
        ext_p[pl.ds(tokens, tokens), cols] = p.astype(BF16)
        ext_g[pl.ds(0, tokens), cols] = cg.astype(BF16)
        return 0

    lax.fori_loop(0, channels // LANES, front, 0)

    to_next = pltpu.make_async_remote_copy(
        src_ref=ext_p.at[pl.ds(tokens, tokens)], dst_ref=ext_p.at[pl.ds(0, tokens)],
        send_sem=sems.at[0], recv_sem=sems.at[1], device_id=(later, rest), device_id_type=MESH)
    to_prev = pltpu.make_async_remote_copy(
        src_ref=ext_g.at[pl.ds(0, tokens)], dst_ref=ext_g.at[pl.ds(tokens, tokens)],
        send_sem=sems.at[2], recv_sem=sems.at[3], device_id=(prev, rest), device_id_type=MESH)

    @pl.when(has_next)
    def _():
        to_next.start()

    @pl.when(has_prev)
    def _():
        to_prev.start()

    @pl.when(jnp.logical_not(has_prev))
    def _():
        ext_p[pl.ds(0, tokens), :] = jnp.zeros((tokens, channels), BF16)

    @pl.when(jnp.logical_not(has_next))
    def _():
        ext_g[pl.ds(tokens, tokens), :] = jnp.zeros((tokens, channels), BF16)

    @pl.when(has_prev)
    def _():
        to_next.wait_recv()

    @pl.when(has_next)
    def _():
        to_prev.wait_recv()

    per_tile = LANES // width
    lane = lax.broadcasted_iota(jnp.int32, (tokens, LANES), 1) // width

    def mixed(rows, ext, first):
        acc = None
        for g in range(per_tile):
            line = jnp.concatenate([rows[g : g + 1], jnp.zeros((1, 2 * tokens - taps_count), F32)], axis=1)
            wide = jnp.broadcast_to(line, (tokens, 2 * tokens))
            toeplitz = pltpu.roll(wide, first, 1, stride=1, stride_axis=0).astype(BF16)
            part = jnp.dot(toeplitz, ext, preferred_element_type=F32)
            acc = part if acc is None else jnp.where(lane == g, part, acc)
        return acc

    def back(at, _):
        cols = pl.ds(pl.multiple_of(at * LANES, LANES), LANES)
        rows = pl.ds(pl.multiple_of(at * per_tile, per_tile), per_tile)
        gain = skip[:, cols]
        conv = mixed(taps_back[rows, :], ext_p[:, cols], 1 + tokens - taps_count) + gain * prod[:, cols]
        pg = mixed(taps[rows, :], ext_g[:, cols], 0) + gain * conv_grad[:, cols]
        out[:, cols] = (query[:, cols] * conv).astype(BF16)
        own = pl.ds(0, tokens)
        filt_grad[0, own, cols] = upstream[:, cols].astype(F32) * conv
        filt_grad[1, own, cols] = pg * value[:, cols]
        filt_grad[2, own, cols] = pg * key[:, cols]
        return 0

    lax.fori_loop(0, channels // LANES, back, 0)

    head = pltpu.make_async_remote_copy(
        src_ref=filt_grad.at[:, pl.ds(0, HEAD)], dst_ref=filt_grad.at[:, pl.ds(tokens, HEAD)],
        send_sem=head_sems.at[0], recv_sem=head_sems.at[1], device_id=(prev, rest), device_id_type=MESH)

    @pl.when(has_prev)
    def _():
        head.start()

    @pl.when(jnp.logical_not(has_next))
    def _():
        filt_grad[:, pl.ds(tokens, HEAD), :] = jnp.zeros((3, HEAD, channels), F32)

    @pl.when(has_next)
    def _():
        head.wait_recv()

    def last(at, _):
        cols = pl.ds(pl.multiple_of(at * LANES, LANES), LANES)
        for i in range(3):
            f = filt_grad[i, :, cols]
            acc = short[pl.ds(i, 1), cols] * f[:tokens]
            for j in range(1, 3):
                acc = acc + short[pl.ds(3 * j + i, 1), cols] * pltpu.roll(f, tokens + HEAD - j, 0)[:tokens]
            grad[i, :, cols] = acc.astype(BF16)
        return 0

    lax.fori_loop(0, channels // LANES, last, 0)

    @pl.when(has_next)
    def _():
        to_next.wait_send()

    @pl.when(has_prev)
    def _():
        to_prev.wait_send()
        head.wait_send()


def hyena(feat, short_filter, long_filter, decay_rate, skip_gain, upstream):
    tokens, channels = upstream.shape
    taps = long_filter * jnp.exp(-decay_rate[:, None] * jnp.arange(long_filter.shape[1]).astype(F32)[None, :])
    width = channels // long_filter.shape[0]
    wide = pltpu.VMEM((tokens, channels), F32)
    return pl.pallas_call(
        functools.partial(hyena_kernel, lax.axis_size("fsdp"), width),
        out_shape=(jax.ShapeDtypeStruct((tokens, channels), BF16), jax.ShapeDtypeStruct((3, tokens, channels), BF16)),
        in_specs=[VMEM] * 6,
        out_specs=(VMEM, VMEM),
        scratch_shapes=[
            pltpu.VMEM((2 * tokens, channels), BF16), pltpu.VMEM((2 * tokens, channels), BF16),
            wide, wide, wide, wide, wide, pltpu.VMEM((3, tokens + HEAD, channels), F32),
            pltpu.SemaphoreType.DMA((4,)), pltpu.SemaphoreType.DMA((2,)),
        ],
        compiler_params=pltpu.CompilerParams(collective_id=1, has_side_effects=True, vmem_limit_bytes=40 * 2**20),
    )(feat, short_filter.reshape(9, channels), taps, taps[:, ::-1], skip_gain[None], upstream)


def remote(src, dst, send, recv, where):
    return pltpu.make_async_remote_copy(
        src_ref=src, dst_ref=dst, send_sem=send, recv_sem=recv, device_id=where, device_id_type=MESH)


class Place:
    def __init__(self, levels):
        self.f = lax.axis_index("fsdp")
        self.t = lax.axis_index("tp")
        self.levels = levels
        self.z, self.y = self.t // 2, lax.rem(self.t, 2)
        self.x, self.core = self.f // 2, lax.rem(self.f, 2)
        self.pair = (self.f, 2 * self.z + 1 - self.y)
        self.up = (self.f, 2 * lax.rem(self.z + 1, levels) + self.y)
        self.down = (self.f, 2 * lax.rem(self.z + levels - 1, levels) + self.y)
        self.twin = (2 * self.x + 1 - self.core, self.t)
        self.across = (2 * (1 - self.x) + self.core, self.t)

    def greet(self):
        barrier = pltpu.get_barrier_semaphore()
        peers = (self.pair, self.up, self.down, self.twin, self.across)
        for peer in peers:
            pl.semaphore_signal(barrier, inc=1, device_id=peer, device_id_type=MESH)
        pl.semaphore_wait(barrier, len(peers))


def features_kernel(
    levels, cuts, x, w, gath, feat,
    wv, rows, mine, to_twin, from_twin, to_far, from_far,
    w_sem, got, pair_sem, up_sem, down_sem, twin_send, twin_got, far_send, far_got,
):
    at = Place(levels)
    blocks, own, depth = x.shape
    tokens, channels = gath.shape[1], w.shape[2]
    span = tokens + HALO
    part = depth // cuts
    loads = [pltpu.make_async_copy(w.at[i], wv.at[i], w_sem.at[i]) for i in range(3)]
    for load in loads:
        load.start()
    gath[:, pl.ds(pl.multiple_of(at.t * own, own), own), :] = x[...]
    at.greet()

    def shard(t, h):
        return gath.at[:, pl.ds(pl.multiple_of(t * own, own), own), pl.ds(h * part, part)]

    def push(t, h, send, where):
        return remote(shard(t, h), shard(t, h), send, got.at[t, h], where)

    def source(k):
        return 2 * (at.z - k) + at.y

    def upward(k, h):
        return push(source(k), h, up_sem.at[k, h], at.up)

    def downward(k, h):
        return push(source(-k), h, down_sem.at[k, h], at.down)

    def sideways(k, h):
        return push(source(k), h, pair_sem.at[k + levels, h], at.pair)

    can_up, can_down = at.z < levels - 1, at.z > 0
    for h in range(cuts):
        @pl.when(can_up)
        def _():
            upward(0, h).start()

        @pl.when(can_down)
        def _():
            downward(0, h).start()

        sideways(0, h).start()
    for k in range(1, levels):
        for h in range(cuts):
            @pl.when(at.z >= k)
            def _():
                sideways(k, h).wait_recv()

                @pl.when(can_up)
                def _():
                    upward(k, h).start()

                sideways(k, h).start()

            @pl.when(at.z + k < levels)
            def _():
                sideways(-k, h).wait_recv()

                @pl.when(can_down)
                def _():
                    downward(k, h).start()

                sideways(-k, h).start()
    for z in range(levels):
        for h in range(cuts):
            push(2 * z + 1 - at.y, h, pair_sem.at[0, 0], at.pair).wait_recv()

    tile = min(256, channels)
    for phase in range(2):
        side = 1 - at.x if phase == 0 else at.x
        for c in range(2):
            block = 2 * side + c
            before = gath[jnp.maximum(block - 1, 0), pl.ds(tokens - HALO, HALO), :]
            rows[pl.ds(c * span, HALO), :] = jnp.where(block > 0, before, jnp.zeros_like(before))
            rows[pl.ds(c * span + HALO, tokens), :] = gath[block]
        for i in range(3):
            if phase == 0:
                loads[i].wait()

            def step(n, _):
                cols = pl.ds(pl.multiple_of(n * tile, tile), tile)
                both = jnp.dot(rows[...], wv[i, :, cols], preferred_element_type=F32)
                low, high = both[:span], both[span:]
                mine[i, :, cols] = jnp.where(at.core == 0, low, high)
                to_twin[phase, i, :, cols] = jnp.where(at.core == 0, high, low).astype(BF16)
                return 0

            lax.fori_loop(0, channels // tile, step, 0)
            swap = remote(
                to_twin.at[phase, i], from_twin.at[phase, i], twin_send.at[phase, i], twin_got.at[phase, i], at.twin)
            swap.start()
            if phase == 0:
                swap.wait_recv()
                to_far[i] = (mine[i] + from_twin[0, i].astype(F32)).astype(BF16)
                remote(to_far.at[i], from_far.at[i], far_send.at[i], far_got.at[i], at.across).start()
    for i in range(3):
        far = remote(to_far.at[i], from_far.at[i], far_send.at[i], far_got.at[i], at.across)
        swap = remote(to_twin.at[1, i], from_twin.at[1, i], twin_send.at[1, i], twin_got.at[1, i], at.twin)
        swap.wait_recv()
        far.wait_recv()
        feat[i] = (mine[i] + from_twin[1, i].astype(F32) + from_far[i].astype(F32)).astype(BF16)

    for i in range(3):
        remote(to_far.at[i], from_far.at[i], far_send.at[i], far_got.at[i], at.across).wait_send()
        for phase in range(2):
            remote(
                to_twin.at[phase, i], from_twin.at[phase, i], twin_send.at[phase, i], twin_got.at[phase, i], at.twin
            ).wait_send()
    for h in range(cuts):
        for k in range(levels):
            @pl.when(jnp.logical_and(can_up, at.z >= k))
            def _():
                upward(k, h).wait_send()

            @pl.when(jnp.logical_and(can_down, at.z + k < levels))
            def _():
                downward(k, h).wait_send()

            @pl.when(at.z >= k)
            def _():
                sideways(k, h).wait_send()

            if k > 0:
                @pl.when(at.z + k < levels)
                def _():
                    sideways(-k, h).wait_send()


def gather_features(x, w, ways):
    blocks, own, depth = x.shape
    channels = w.shape[2]
    levels, cuts = ways // 2, 2
    tokens = own * ways
    span = tokens + HALO
    half = pltpu.VMEM((3, span, channels), BF16)
    twice = pltpu.VMEM((2, 3, span, channels), BF16)
    dma = pltpu.SemaphoreType.DMA
    return pl.pallas_call(
        functools.partial(features_kernel, levels, cuts),
        out_shape=(
            jax.ShapeDtypeStruct((blocks, tokens, depth), BF16), jax.ShapeDtypeStruct((3, span, channels), BF16)),
        in_specs=[VMEM, pl.BlockSpec(memory_space=pl.ANY)],
        out_specs=(VMEM, VMEM),
        scratch_shapes=[
            pltpu.VMEM(w.shape, BF16), pltpu.VMEM((2 * span, depth), BF16),
            pltpu.VMEM((3, span, channels), F32), twice, twice, half, half,
            dma((3,)), dma((ways, cuts)), dma((2 * levels, cuts)), dma((levels, cuts)), dma((levels, cuts)),
            dma((2, 3)), dma((2, 3)), dma((3,)), dma((3,)),
        ],
        compiler_params=pltpu.CompilerParams(collective_id=0, has_side_effects=True, vmem_limit_bytes=48 * 2**20),
    )(x, w)


def input_grad_kernel(
    levels, g, w, grads, out,
    wv, partial, side_in, up_in, down_in, staged, total,
    w_sem, twin_send, twin_got, far_send, far_got, pass_send, pass_got,
    side_send, side_got, line_send, up_got, down_got,
):
    at = Place(levels)
    blocks, own, depth = out.shape
    channels, tokens = g.shape[2], g.shape[1]
    loads = [pltpu.make_async_copy(w.at[i], wv.at[i], w_sem.at[i]) for i in range(3)]
    for load in loads:
        load.start()
    for i in range(3):
        grads[i, at.f] = g[i]
    at.greet()
    there = 2 * (1 - at.x) + at.core

    def to_far(i):
        return remote(grads.at[i, at.f], grads.at[i, at.f], far_send.at[i], far_got.at[i], at.across)

    def to_twin(i):
        return remote(grads.at[i, at.f], grads.at[i, at.f], twin_send.at[i], twin_got.at[i], at.twin)

    def passed(i):
        return remote(grads.at[i, there], grads.at[i, there], pass_send.at[i], pass_got.at[i], at.twin)

    for i in range(3):
        to_far(i).start()
        to_twin(i).start()

    tile = min(256, depth)

    def multiply(half):
        side = at.x if half == 0 else 1 - at.x

        def step(n, _):
            cols = pl.ds(pl.multiple_of(n * tile, tile), tile)
            acc = None
            for i in range(3):
                pair = grads[i, pl.ds(2 * side, 2)].reshape(2 * tokens, channels)
                term = lax.dot_general(pair, wv[i, cols, :], (((1,), (1,)), ((), ())), preferred_element_type=F32)
                acc = term if acc is None else acc + term
            partial[half, :, :, cols] = acc.astype(BF16).reshape(2, tokens, tile)
            return 0

        lax.fori_loop(0, depth // tile, step, 0)

    def piece(half, t):
        return partial.at[half, :, pl.ds(pl.multiple_of(t * own, own), own)]

    def sideways(half, z):
        return remote(
            piece(half, 2 * z + 1 - at.y), side_in.at[half, z], side_send.at[half, z], side_got.at[half, z], at.pair)

    def upward(half, z):
        return remote(staged.at[half, z], up_in.at[half, z], line_send.at[half, z], up_got.at[half, z], at.up)

    def downward(half, z):
        return remote(staged.at[half, z], down_in.at[half, z], line_send.at[half, z], down_got.at[half, z], at.down)

    def own_sum(half, z):
        sideways(half, z).wait_recv()
        return piece(half, 2 * z + at.y)[...].astype(F32) + side_in[half, z].astype(F32)

    def start_side(half):
        for k in range(levels - 1, 0, -1):
            @pl.when(at.z + k < levels)
            def _():
                sideways(half, at.z + k).start()

            @pl.when(at.z >= k)
            def _():
                sideways(half, at.z - k).start()

        sideways(half, at.z).start()

    def line(half, k):
        @pl.when(at.z + k < levels)
        def _():
            z = at.z + k
            staged[half, z] = own_sum(half, z).astype(BF16)

            @pl.when(at.z > 0)
            def _():
                upward(half, z).wait_recv()
                staged[half, z] = (staged[half, z].astype(F32) + up_in[half, z].astype(F32)).astype(BF16)

            upward(half, z).start()

        @pl.when(at.z >= k)
        def _():
            z = at.z - k
            staged[half, z] = own_sum(half, z).astype(BF16)

            @pl.when(at.z < levels - 1)
            def _():
                downward(half, z).wait_recv()
                staged[half, z] = (staged[half, z].astype(F32) + down_in[half, z].astype(F32)).astype(BF16)

            downward(half, z).start()

    def finish(half):
        z = at.z
        side = at.x if half == 0 else 1 - at.x
        total[...] = own_sum(half, z)

        @pl.when(z > 0)
        def _():
            upward(half, z).wait_recv()
            total[...] += up_in[half, z].astype(F32)

        @pl.when(z < levels - 1)
        def _():
            downward(half, z).wait_recv()
            total[...] += down_in[half, z].astype(F32)

        out[pl.ds(2 * side, 2)] = total[...].astype(BF16)

    for i in range(3):
        loads[i].wait()
        to_twin(i).wait_recv()
    multiply(0)
    start_side(0)
    for i in range(3):
        if i < levels - 1:
            line(0, levels - 1 - i)
        to_far(i).wait_recv()
        passed(i).start()
    for k in range(levels - 4, 0, -1):
        line(0, k)
    for i in range(3):
        passed(i).wait_recv()
    multiply(1)
    start_side(1)
    finish(0)
    for k in range(levels - 1, 0, -1):
        line(1, k)
    finish(1)

    for i in range(3):
        to_far(i).wait_send()
        to_twin(i).wait_send()
        passed(i).wait_send()
    for half in range(2):
        for z in range(levels):
            sideways(half, z).wait_send()

            @pl.when(z != at.z)
            def _():
                upward(half, z).wait_send()


def input_product(g, w, ways):
    blocks, tokens, channels = 4, g.shape[1], g.shape[2]
    depth = w.shape[1]
    levels, own = ways // 2, tokens // ways
    pieces = pltpu.VMEM((2, levels, 2, own, depth), BF16)
    dma = pltpu.SemaphoreType.DMA
    lines = dma((2, levels))
    return pl.pallas_call(
        functools.partial(input_grad_kernel, levels),
        out_shape=(
            jax.ShapeDtypeStruct((3, blocks, tokens, channels), BF16),
            jax.ShapeDtypeStruct((blocks, own, depth), BF16)),
        in_specs=[VMEM, pl.BlockSpec(memory_space=pl.ANY)],
        out_specs=(VMEM, VMEM),
        scratch_shapes=[
            pltpu.VMEM(w.shape, BF16), pltpu.VMEM((2, 2, tokens, depth), BF16), pieces, pieces, pieces, pieces,
            pltpu.VMEM((2, own, depth), F32),
            dma((3,)), dma((3,)), dma((3,)), dma((3,)), dma((3,)), dma((3,)), dma((3,)),
            lines, lines, lines, lines, lines,
        ],
        compiler_params=pltpu.CompilerParams(collective_id=2, has_side_effects=True, vmem_limit_bytes=48 * 2**20),
    )(g, w)


def weight_kernel(x, g, out):
    out[...] = lax.dot_general(x[...], g[...], (((0,), (0,)), ((), ())), preferred_element_type=F32).astype(BF16)


def weight_product(x, grads):
    rows, depth = x.shape
    channels = grads.shape[2]
    step = min(512, depth)
    return pl.pallas_call(
        weight_kernel,
        grid=(depth // step, 3),
        out_shape=jax.ShapeDtypeStruct((3, depth, channels), BF16),
        in_specs=[
            pl.BlockSpec((rows, step), lambda d, i: (0, d)),
            pl.BlockSpec((None, rows, channels), lambda d, i: (i, 0, 0)),
        ],
        out_specs=pl.BlockSpec((None, step, channels), lambda d, i: (i, d, 0)),
        compiler_params=pltpu.CompilerParams(vmem_limit_bytes=40 * 2**20),
        cost_estimate=pl.CostEstimate(
            flops=6 * rows * depth * channels, bytes_accessed=2 * 3 * depth * channels, transcendentals=0),
    )(x, grads)


def shards_general(inputs, featurizer, short_filter, long_filter, decay_rate, skip_gain, output_grad):
    weights = featurizer.transpose(1, 0, 2)
    gathered = lax.all_gather(inputs.transpose(1, 0, 2), "tp", axis=1, tiled=True)
    blocks, tokens, depth = gathered.shape
    channels = weights.shape[2]
    border = jnp.zeros((1, HALO, depth), BF16)
    earlier = jnp.concatenate([border, gathered[: blocks - 1, tokens - HALO :]], axis=0)
    extended = jnp.concatenate([earlier, gathered], axis=1).reshape(blocks * (tokens + HALO), depth)
    feats = []
    for i in range(3):
        part = jnp.dot(extended, weights[i], preferred_element_type=F32).astype(BF16)
        part = part.reshape(blocks, tokens + HALO, channels)
        swapped = lax.all_to_all(part, "fsdp", split_axis=0, concat_axis=0, tiled=True)
        feats.append(jnp.sum(swapped.astype(F32), axis=0).astype(BF16))
    out, own_grad = hyena(
        jnp.stack(feats), short_filter, long_filter, decay_rate, skip_gain, output_grad.reshape(tokens, channels))
    grads = lax.all_gather(own_grad, "fsdp", axis=1, tiled=True)
    turned = grads.reshape(3, blocks, tokens, channels).transpose(0, 2, 1, 3).reshape(grads.shape)
    part = None
    for i in range(3):
        term = lax.dot_general(turned[i], weights[i], (((1,), (1,)), ((), ())), preferred_element_type=F32)
        part = term if part is None else part + term
    weight_grad = weight_product(gathered.reshape(blocks * tokens, depth), grads)
    input_grad = lax.psum_scatter(
        part.astype(BF16).reshape(tokens, blocks, depth), "tp", scatter_dimension=0, tiled=True)
    return out.reshape(output_grad.shape), input_grad, weight_grad.transpose(1, 0, 2)


def shards(inputs, featurizer, short_filter, long_filter, decay_rate, skip_gain, output_grad):
    ways = lax.axis_size("tp")
    if inputs.shape[0] % 16 or lax.axis_size("fsdp") != 4 or ways % 4:
        return shards_general(inputs, featurizer, short_filter, long_filter, decay_rate, skip_gain, output_grad)
    weights = featurizer.transpose(1, 0, 2)
    gathered, feats = gather_features(inputs.transpose(1, 0, 2), weights, ways)
    blocks, tokens, depth = gathered.shape
    channels = weights.shape[2]
    out, own_grad = hyena(
        feats, short_filter, long_filter, decay_rate, skip_gain, output_grad.reshape(tokens, channels))
    grads, input_grad = input_product(own_grad, weights, ways)
    weight_grad = weight_product(
        gathered.reshape(blocks * tokens, depth), grads.reshape(3, blocks * tokens, channels))
    return out.reshape(output_grad.shape), input_grad.transpose(1, 0, 2), weight_grad.transpose(1, 0, 2)


def solution(mesh):
    in_specs = (
        P("tp", None, "fsdp"),
        P("fsdp", None, "tp"),
        P(None, None, "tp"),
        P("tp", None),
        P("tp"),
        P("tp"),
        P(None, "fsdp", "tp"),
    )
    out_specs = (P(None, "fsdp", "tp"), P("tp", None, "fsdp"), P("fsdp", None, "tp"))
    return jax.shard_map(shards, mesh=mesh, in_specs=in_specs, out_specs=out_specs, check_vma=False)
```

```python
import functools

import jax
import jax.numpy as jnp
from jax import lax
from jax.experimental import pallas as pl
from jax.experimental.pallas import tpu as pltpu
from jax.sharding import PartitionSpec as P

F32 = jnp.float32
BF16 = jnp.bfloat16
MESH = pl.DeviceIdType.MESH
VMEM = pl.BlockSpec(memory_space=pltpu.VMEM)
LANES = 128
HALO = 16
HEAD = 8


def hyena_kernel(
    blocks, width, feat, short, taps, taps_back, skip, upstream, out, grad,
    ext_p, ext_g, query, key, value, prod, conv_grad, filt_grad, sems, head_sems,
):
    me = lax.axis_index("fsdp")
    rest = lax.axis_index("tp")
    tokens, channels = out.shape
    taps_count = taps.shape[1]
    has_prev = me > 0
    has_next = me < blocks - 1
    prev = jnp.maximum(me - 1, 0)
    later = jnp.minimum(me + 1, blocks - 1)
    barrier = pltpu.get_barrier_semaphore()

    for peer in (lax.rem(me + 1, blocks), lax.rem(me + blocks - 1, blocks)):
        pl.semaphore_signal(barrier, inc=1, device_id=(peer, rest), device_id_type=MESH)
    pl.semaphore_wait(barrier, 2)

    def front(at, _):
        cols = pl.ds(pl.multiple_of(at * LANES, LANES), LANES)
        parts = []
        for i in range(3):
            f = feat[i, :, cols].astype(F32)
            acc = short[pl.ds(i, 1), cols] * f[HALO:]
            for j in range(1, 3):
                acc = acc + short[pl.ds(3 * j + i, 1), cols] * pltpu.roll(f, j, 0)[HALO:]
            parts.append(acc)
        p = parts[1] * parts[2]
        cg = upstream[:, cols].astype(F32) * parts[0]
        query[:, cols] = parts[0]
        key[:, cols] = parts[1]
        value[:, cols] = parts[2]
        prod[:, cols] = p
        conv_grad[:, cols] = cg
        ext_p[pl.ds(tokens, tokens), cols] = p.astype(BF16)
        ext_g[pl.ds(0, tokens), cols] = cg.astype(BF16)
        return 0

    lax.fori_loop(0, channels // LANES, front, 0)

    to_next = pltpu.make_async_remote_copy(
        src_ref=ext_p.at[pl.ds(tokens, tokens)], dst_ref=ext_p.at[pl.ds(0, tokens)],
        send_sem=sems.at[0], recv_sem=sems.at[1], device_id=(later, rest), device_id_type=MESH)
    to_prev = pltpu.make_async_remote_copy(
        src_ref=ext_g.at[pl.ds(0, tokens)], dst_ref=ext_g.at[pl.ds(tokens, tokens)],
        send_sem=sems.at[2], recv_sem=sems.at[3], device_id=(prev, rest), device_id_type=MESH)

    @pl.when(has_next)
    def _():
        to_next.start()

    @pl.when(has_prev)
    def _():
        to_prev.start()

    @pl.when(jnp.logical_not(has_prev))
    def _():
        ext_p[pl.ds(0, tokens), :] = jnp.zeros((tokens, channels), BF16)

    @pl.when(jnp.logical_not(has_next))
    def _():
        ext_g[pl.ds(tokens, tokens), :] = jnp.zeros((tokens, channels), BF16)

    @pl.when(has_prev)
    def _():
        to_next.wait_recv()

    @pl.when(has_next)
    def _():
        to_prev.wait_recv()

    per_tile = LANES // width
    lane = lax.broadcasted_iota(jnp.int32, (tokens, LANES), 1) // width

    def mixed(rows, ext, first):
        acc = None
        for g in range(per_tile):
            line = jnp.concatenate([rows[g : g + 1], jnp.zeros((1, 2 * tokens - taps_count), F32)], axis=1)
            wide = jnp.broadcast_to(line, (tokens, 2 * tokens))
            toeplitz = pltpu.roll(wide, first, 1, stride=1, stride_axis=0).astype(BF16)
            part = jnp.dot(toeplitz, ext, preferred_element_type=F32)
            acc = part if acc is None else jnp.where(lane == g, part, acc)
        return acc

    def back(at, _):
        cols = pl.ds(pl.multiple_of(at * LANES, LANES), LANES)
        rows = pl.ds(pl.multiple_of(at * per_tile, per_tile), per_tile)
        gain = skip[:, cols]
        conv = mixed(taps_back[rows, :], ext_p[:, cols], 1 + tokens - taps_count) + gain * prod[:, cols]
        pg = mixed(taps[rows, :], ext_g[:, cols], 0) + gain * conv_grad[:, cols]
        out[:, cols] = (query[:, cols] * conv).astype(BF16)
        own = pl.ds(0, tokens)
        filt_grad[0, own, cols] = upstream[:, cols].astype(F32) * conv
        filt_grad[1, own, cols] = pg * value[:, cols]
        filt_grad[2, own, cols] = pg * key[:, cols]
        return 0

    lax.fori_loop(0, channels // LANES, back, 0)

    head = pltpu.make_async_remote_copy(
        src_ref=filt_grad.at[:, pl.ds(0, HEAD)], dst_ref=filt_grad.at[:, pl.ds(tokens, HEAD)],
        send_sem=head_sems.at[0], recv_sem=head_sems.at[1], device_id=(prev, rest), device_id_type=MESH)

    @pl.when(has_prev)
    def _():
        head.start()

    @pl.when(jnp.logical_not(has_next))
    def _():
        filt_grad[:, pl.ds(tokens, HEAD), :] = jnp.zeros((3, HEAD, channels), F32)

    @pl.when(has_next)
    def _():
        head.wait_recv()

    def last(at, _):
        cols = pl.ds(pl.multiple_of(at * LANES, LANES), LANES)
        for i in range(3):
            f = filt_grad[i, :, cols]
            acc = short[pl.ds(i, 1), cols] * f[:tokens]
            for j in range(1, 3):
                acc = acc + short[pl.ds(3 * j + i, 1), cols] * pltpu.roll(f, tokens + HEAD - j, 0)[:tokens]
            grad[i, :, cols] = acc.astype(BF16)
        return 0

    lax.fori_loop(0, channels // LANES, last, 0)

    @pl.when(has_next)
    def _():
        to_next.wait_send()

    @pl.when(has_prev)
    def _():
        to_prev.wait_send()
        head.wait_send()


def hyena(feat, short_filter, long_filter, decay_rate, skip_gain, upstream):
    tokens, channels = upstream.shape
    taps = long_filter * jnp.exp(-decay_rate[:, None] * jnp.arange(long_filter.shape[1]).astype(F32)[None, :])
    width = channels // long_filter.shape[0]
    wide = pltpu.VMEM((tokens, channels), F32)
    return pl.pallas_call(
        functools.partial(hyena_kernel, lax.axis_size("fsdp"), width),
        out_shape=(jax.ShapeDtypeStruct((tokens, channels), BF16), jax.ShapeDtypeStruct((3, tokens, channels), BF16)),
        in_specs=[VMEM] * 6,
        out_specs=(VMEM, VMEM),
        scratch_shapes=[
            pltpu.VMEM((2 * tokens, channels), BF16), pltpu.VMEM((2 * tokens, channels), BF16),
            wide, wide, wide, wide, wide, pltpu.VMEM((3, tokens + HEAD, channels), F32),
            pltpu.SemaphoreType.DMA((4,)), pltpu.SemaphoreType.DMA((2,)),
        ],
        compiler_params=pltpu.CompilerParams(collective_id=1, has_side_effects=True, vmem_limit_bytes=40 * 2**20),
    )(feat, short_filter.reshape(9, channels), taps, taps[:, ::-1], skip_gain[None], upstream)


def remote(src, dst, send, recv, where):
    return pltpu.make_async_remote_copy(
        src_ref=src, dst_ref=dst, send_sem=send, recv_sem=recv, device_id=where, device_id_type=MESH)


class Place:
    def __init__(self, levels):
        self.f = lax.axis_index("fsdp")
        self.t = lax.axis_index("tp")
        self.levels = levels
        self.z, self.y = self.t // 2, lax.rem(self.t, 2)
        self.x, self.core = self.f // 2, lax.rem(self.f, 2)
        self.pair = (self.f, 2 * self.z + 1 - self.y)
        self.up = (self.f, 2 * lax.rem(self.z + 1, levels) + self.y)
        self.down = (self.f, 2 * lax.rem(self.z + levels - 1, levels) + self.y)
        self.twin = (2 * self.x + 1 - self.core, self.t)
        self.across = (2 * (1 - self.x) + self.core, self.t)

    def nearest(self, step):
        levels, z = self.levels, self.z
        paired = jnp.minimum(z, levels - 1 - z)
        near = (step + 1) // 2 * (1 if step % 2 == 0 else -1)
        far = (step - paired) * jnp.where(z < levels - 1 - z, 1, -1)
        return z + jnp.where(step <= 2 * paired, near, far)

    def greet(self):
        barrier = pltpu.get_barrier_semaphore()
        peers = (self.pair, self.up, self.down, self.twin, self.across)
        for peer in peers:
            pl.semaphore_signal(barrier, inc=1, device_id=peer, device_id_type=MESH)
        pl.semaphore_wait(barrier, len(peers))


def features_kernel(
    levels, cuts, x, w, turned, feat,
    gath, wv, result, mine, total, to_twin, from_twin, to_far, from_far,
    w_sem, got, pair_sem, up_sem, down_sem, twin_send, twin_got, far_send, far_got, edge_send, edge_got,
):
    at = Place(levels)
    blocks, own, depth = x.shape
    tokens, channels = gath.shape[1], w.shape[2]
    part = depth // cuts
    both = 2 * own
    loads = [pltpu.make_async_copy(w.at[i], wv.at[i], w_sem.at[i]) for i in range(3)]
    for load in loads:
        load.start()
    gath[:, pl.ds(pl.multiple_of(at.t * own, own), own), :] = x[...]
    at.greet()

    def shard(t, h):
        return gath.at[:, pl.ds(pl.multiple_of(t * own, own), own), pl.ds(h * part, part)]

    def push(t, h, send, where):
        return remote(shard(t, h), shard(t, h), send, got.at[t, h], where)

    def source(k):
        return 2 * (at.z - k) + at.y

    def upward(k, h):
        return push(source(k), h, up_sem.at[k, h], at.up)

    def downward(k, h):
        return push(source(-k), h, down_sem.at[k, h], at.down)

    def sideways(k, h):
        return push(source(k), h, pair_sem.at[k + levels, h], at.pair)

    can_up, can_down = at.z < levels - 1, at.z > 0
    for h in range(cuts):
        @pl.when(can_up)
        def _():
            upward(0, h).start()

        @pl.when(can_down)
        def _():
            downward(0, h).start()

        sideways(0, h).start()

    tile = min(256, channels)
    main, edge = pl.ds(0, both), pl.ds(both, HALO)
    last = levels - 1

    def swap(n, i):
        return remote(to_twin.at[n, i], from_twin.at[n, i], twin_send.at[n, i], twin_got.at[n, i], at.twin)

    def far(i, z):
        spot = pl.ds(pl.multiple_of(HALO + z * both, HALO), both)
        return remote(to_far.at[i, spot], from_far.at[i, spot], far_send.at[i, z], far_got.at[i, z], at.across)

    def far_edge(i):
        spot = pl.ds(0, HALO)
        return remote(to_far.at[i, spot], from_far.at[i, spot], edge_send.at[i], edge_got.at[i], at.across)

    def passed_on(n, i):
        z = at.nearest(n)
        spot = pl.ds(pl.multiple_of(HALO + z * both, HALO), both)
        slot = (3 * n + i) % 2
        swap(n, i).wait_recv()
        to_far[i, spot] = (mine[slot, 0, main] + from_twin[n, i, 0, main].astype(F32)).astype(BF16)
        far(i, z).start()
        total[i, spot] = mine[slot, 1, main] + from_twin[n, i, 1, main].astype(F32)

        @pl.when(z == last)
        def _():
            spot = pl.ds(0, HALO)
            to_far[i, spot] = (mine[slot, 0, edge] + from_twin[n, i, 0, edge].astype(F32)).astype(BF16)
            far_edge(i).start()
            total[i, spot] = mine[slot, 1, edge] + from_twin[n, i, 1, edge].astype(F32)

    def group(n):
        z = at.nearest(n)
        for h in range(cuts):
            push(2 * z + 1 - at.y, h, pair_sem.at[0, 0], at.pair).wait_recv()
        spot = pl.ds(pl.multiple_of(z * both, both), both)
        for i in range(3):
            if n == 0:
                loads[i].wait()

            def step(m, _):
                cols = pl.ds(pl.multiple_of(m * tile, tile), tile)
                lines = gath[:, spot, :].reshape(blocks * both, depth)
                term = jnp.dot(lines, wv[i, :, cols], preferred_element_type=F32)
                result[:, :, cols] = term.reshape(blocks, both, tile)
                return 0

            lax.fori_loop(0, channels // tile, step, 0)
            slot = (3 * n + i) % 2
            for phase in range(2):
                side = 1 - at.x if phase == 0 else at.x
                for other in range(2):
                    block = 2 * side + (1 - at.core if other else at.core)
                    before = result[jnp.maximum(block - 1, 0), pl.ds(both - HALO, HALO), :]
                    before = jnp.where(block > 0, before, jnp.zeros_like(before))
                    if other:
                        to_twin[n, i, phase, main] = result[block].astype(BF16)
                        to_twin[n, i, phase, edge] = before.astype(BF16)
                    else:
                        mine[slot, phase, main] = result[block]
                        mine[slot, phase, edge] = before
            swap(n, i).start()
            if n + i > 0:
                passed_on(n if i > 0 else n - 1, i - 1 if i > 0 else 2)

    for k in range(1, levels):
        for h in range(cuts):
            @pl.when(at.z >= k)
            def _():
                sideways(k, h).wait_recv()

                @pl.when(can_up)
                def _():
                    upward(k, h).start()

                sideways(k, h).start()

            @pl.when(at.z + k < levels)
            def _():
                sideways(-k, h).wait_recv()

                @pl.when(can_down)
                def _():
                    downward(k, h).start()

                sideways(-k, h).start()
        group(k - 1)
    group(levels - 1)
    passed_on(levels - 1, 2)
    for n in range(depth // tile):
        cols = pl.ds(n * tile, tile)
        turned[cols, :] = gath[:, :, cols].reshape(blocks * tokens, tile).T
    for i in range(3):
        for z in range(levels):
            far(i, z).wait_recv()
        far_edge(i).wait_recv()
        feat[i] = (total[i] + from_far[i].astype(F32)).astype(BF16)

    for i in range(3):
        for n in range(levels):
            far(i, n).wait_send()
            swap(n, i).wait_send()
        far_edge(i).wait_send()
    for h in range(cuts):
        for k in range(levels):
            @pl.when(jnp.logical_and(can_up, at.z >= k))
            def _():
                upward(k, h).wait_send()

            @pl.when(jnp.logical_and(can_down, at.z + k < levels))
            def _():
                downward(k, h).wait_send()

            @pl.when(at.z >= k)
            def _():
                sideways(k, h).wait_send()

            if k > 0:
                @pl.when(at.z + k < levels)
                def _():
                    sideways(-k, h).wait_send()


def gather_features(x, w, ways):
    blocks, own, depth = x.shape
    channels = w.shape[2]
    levels, cuts = ways // 2, 2
    tokens = own * ways
    span = tokens + HALO
    half = pltpu.VMEM((3, span, channels), BF16)
    swaps = pltpu.VMEM((levels, 3, 2, 2 * own + HALO, channels), BF16)
    dma = pltpu.SemaphoreType.DMA
    return pl.pallas_call(
        functools.partial(features_kernel, levels, cuts),
        out_shape=(
            jax.ShapeDtypeStruct((depth, blocks * tokens), BF16), jax.ShapeDtypeStruct((3, span, channels), BF16)),
        in_specs=[VMEM, pl.BlockSpec(memory_space=pl.ANY)],
        out_specs=(VMEM, VMEM),
        scratch_shapes=[
            pltpu.VMEM((blocks, tokens, depth), BF16), pltpu.VMEM(w.shape, BF16),
            pltpu.VMEM((blocks, 2 * own, channels), F32), pltpu.VMEM((2, 2, 2 * own + HALO, channels), F32),
            pltpu.VMEM((3, span, channels), F32), swaps, swaps, half, half,
            dma((3,)), dma((ways, cuts)), dma((2 * levels, cuts)), dma((levels, cuts)), dma((levels, cuts)),
            dma((levels, 3)), dma((levels, 3)), dma((3, levels)), dma((3, levels)), dma((3,)), dma((3,)),
        ],
        compiler_params=pltpu.CompilerParams(collective_id=0, has_side_effects=True, vmem_limit_bytes=48 * 2**20),
    )(x, w)


def input_grad_kernel(
    levels, g, w, grads, out,
    wv, partial, side_in, up_in, down_in, staged, total,
    w_sem, twin_send, twin_got, far_send, far_got, pass_send, pass_got,
    side_send, side_got, line_send, up_got, down_got,
):
    at = Place(levels)
    blocks, own, depth = out.shape
    channels, tokens = g.shape[2], g.shape[1]
    loads = [pltpu.make_async_copy(w.at[i], wv.at[i], w_sem.at[i]) for i in range(3)]
    for load in loads:
        load.start()
    for i in range(3):
        grads[i, at.f] = g[i]
    at.greet()
    there = 2 * (1 - at.x) + at.core
    both = 2 * own

    def level(step):
        return at.nearest(levels - 1 - step)

    def strip(block, z):
        return grads.at[:, block, pl.ds(pl.multiple_of(z * both, both), both)]

    def to_far(z):
        return remote(strip(at.f, z), strip(at.f, z), far_send.at[z], far_got.at[z], at.across)

    def to_twin(i):
        return remote(grads.at[i, at.f], grads.at[i, at.f], twin_send.at[i], twin_got.at[i], at.twin)

    def passed(z):
        return remote(strip(there, z), strip(there, z), pass_send.at[z], pass_got.at[z], at.twin)

    for step in range(levels):
        to_far(level(step)).start()
    for i in range(3):
        to_twin(i).start()

    tile = min(256, depth)

    def multiply(half, start, count):
        side = at.x if half == 0 else 1 - at.x
        span = pl.ds(start, count)

        def step(n, _):
            cols = pl.ds(pl.multiple_of(n * tile, tile), tile)
            acc = None
            for i in range(3):
                lines = grads[i, pl.ds(2 * side, 2), span].reshape(2 * count, channels)
                term = lax.dot_general(lines, wv[i, cols, :], (((1,), (1,)), ((), ())), preferred_element_type=F32)
                acc = term if acc is None else acc + term
            partial[half, :, span, cols] = acc.astype(BF16).reshape(2, count, tile)
            return 0

        lax.fori_loop(0, depth // tile, step, 0)

    def piece(half, t):
        return partial.at[half, :, pl.ds(pl.multiple_of(t * own, own), own)]

    def sideways(half, z):
        return remote(
            piece(half, 2 * z + 1 - at.y), side_in.at[half, z], side_send.at[half, z], side_got.at[half, z], at.pair)

    def upward(half, z):
        return remote(staged.at[half, z], up_in.at[half, z], line_send.at[half, z], up_got.at[half, z], at.up)

    def downward(half, z):
        return remote(staged.at[half, z], down_in.at[half, z], line_send.at[half, z], down_got.at[half, z], at.down)

    def own_sum(half, z):
        sideways(half, z).wait_recv()
        return piece(half, 2 * z + at.y)[...].astype(F32) + side_in[half, z].astype(F32)

    def line(half, z):
        staged[half, z] = own_sum(half, z).astype(BF16)

        @pl.when(z > at.z)
        def _():
            @pl.when(at.z > 0)
            def _():
                upward(half, z).wait_recv()
                staged[half, z] = (staged[half, z].astype(F32) + up_in[half, z].astype(F32)).astype(BF16)

            upward(half, z).start()

        @pl.when(z < at.z)
        def _():
            @pl.when(at.z < levels - 1)
            def _():
                downward(half, z).wait_recv()
                staged[half, z] = (staged[half, z].astype(F32) + down_in[half, z].astype(F32)).astype(BF16)

            downward(half, z).start()

    def finish(half):
        z = at.z
        side = at.x if half == 0 else 1 - at.x
        total[...] = own_sum(half, z)

        @pl.when(z > 0)
        def _():
            upward(half, z).wait_recv()
            total[...] += up_in[half, z].astype(F32)

        @pl.when(z < levels - 1)
        def _():
            downward(half, z).wait_recv()
            total[...] += down_in[half, z].astype(F32)

        out[pl.ds(2 * side, 2)] = total[...].astype(BF16)

    for i in range(3):
        loads[i].wait()
        to_twin(i).wait_recv()
    multiply(0, 0, tokens)
    for step in range(levels):
        sideways(0, level(step)).start()
    for step in range(levels):
        z = level(step)
        to_far(z).wait_recv()
        passed(z).start()
        if step < levels - 1:
            line(0, z)
        passed(z).wait_recv()
        multiply(1, pl.multiple_of(z * both, both), both)
        sideways(1, z).start()
        if step > 0:
            line(1, level(step - 1))
    finish(0)
    finish(1)

    for i in range(3):
        to_twin(i).wait_send()
    for z in range(levels):
        to_far(z).wait_send()
        passed(z).wait_send()
        for half in range(2):
            sideways(half, z).wait_send()

            @pl.when(z != at.z)
            def _():
                upward(half, z).wait_send()


def input_product(g, w, ways):
    blocks, tokens, channels = 4, g.shape[1], g.shape[2]
    depth = w.shape[1]
    levels, own = ways // 2, tokens // ways
    pieces = pltpu.VMEM((2, levels, 2, own, depth), BF16)
    dma = pltpu.SemaphoreType.DMA
    lines = dma((2, levels))
    return pl.pallas_call(
        functools.partial(input_grad_kernel, levels),
        out_shape=(
            jax.ShapeDtypeStruct((3, blocks, tokens, channels), BF16),
            jax.ShapeDtypeStruct((blocks, own, depth), BF16)),
        in_specs=[VMEM, pl.BlockSpec(memory_space=pl.ANY)],
        out_specs=(VMEM, VMEM),
        scratch_shapes=[
            pltpu.VMEM(w.shape, BF16), pltpu.VMEM((2, 2, tokens, depth), BF16), pieces, pieces, pieces, pieces,
            pltpu.VMEM((2, own, depth), F32),
            dma((3,)), dma((3,)), dma((3,)), dma((levels,)), dma((levels,)), dma((levels,)), dma((levels,)),
            lines, lines, lines, lines, lines,
        ],
        compiler_params=pltpu.CompilerParams(collective_id=2, has_side_effects=True, vmem_limit_bytes=48 * 2**20),
    )(g, w)


def weight_kernel(x, g, out):
    out[...] = jnp.dot(x[...], g[...], preferred_element_type=F32).astype(BF16)


def weight_product(x, grads):
    depth, rows = x.shape
    channels = grads.shape[2]
    step = min(512, depth)
    return pl.pallas_call(
        weight_kernel,
        grid=(depth // step, 3),
        out_shape=jax.ShapeDtypeStruct((3, depth, channels), BF16),
        in_specs=[
            pl.BlockSpec((step, rows), lambda d, i: (d, 0)),
            pl.BlockSpec((None, rows, channels), lambda d, i: (i, 0, 0)),
        ],
        out_specs=pl.BlockSpec((None, step, channels), lambda d, i: (i, d, 0)),
        compiler_params=pltpu.CompilerParams(vmem_limit_bytes=40 * 2**20),
        cost_estimate=pl.CostEstimate(
            flops=6 * rows * depth * channels, bytes_accessed=2 * 3 * depth * channels, transcendentals=0),
    )(x, grads)


def shards_general(inputs, featurizer, short_filter, long_filter, decay_rate, skip_gain, output_grad):
    weights = featurizer.transpose(1, 0, 2)
    gathered = lax.all_gather(inputs.transpose(1, 0, 2), "tp", axis=1, tiled=True)
    blocks, tokens, depth = gathered.shape
    channels = weights.shape[2]
    border = jnp.zeros((1, HALO, depth), BF16)
    earlier = jnp.concatenate([border, gathered[: blocks - 1, tokens - HALO :]], axis=0)
    extended = jnp.concatenate([earlier, gathered], axis=1).reshape(blocks * (tokens + HALO), depth)
    feats = []
    for i in range(3):
        part = jnp.dot(extended, weights[i], preferred_element_type=F32).astype(BF16)
        part = part.reshape(blocks, tokens + HALO, channels)
        swapped = lax.all_to_all(part, "fsdp", split_axis=0, concat_axis=0, tiled=True)
        feats.append(jnp.sum(swapped.astype(F32), axis=0).astype(BF16))
    out, own_grad = hyena(
        jnp.stack(feats), short_filter, long_filter, decay_rate, skip_gain, output_grad.reshape(tokens, channels))
    grads = lax.all_gather(own_grad, "fsdp", axis=1, tiled=True)
    turned = grads.reshape(3, blocks, tokens, channels).transpose(0, 2, 1, 3).reshape(grads.shape)
    part = None
    for i in range(3):
        term = lax.dot_general(turned[i], weights[i], (((1,), (1,)), ((), ())), preferred_element_type=F32)
        part = term if part is None else part + term
    weight_grad = weight_product(gathered.reshape(blocks * tokens, depth).T, grads)
    input_grad = lax.psum_scatter(
        part.astype(BF16).reshape(tokens, blocks, depth), "tp", scatter_dimension=0, tiled=True)
    return out.reshape(output_grad.shape), input_grad, weight_grad.transpose(1, 0, 2)


def shards(inputs, featurizer, short_filter, long_filter, decay_rate, skip_gain, output_grad):
    ways = lax.axis_size("tp")
    if inputs.shape[0] % 16 or lax.axis_size("fsdp") != 4 or ways % 4:
        return shards_general(inputs, featurizer, short_filter, long_filter, decay_rate, skip_gain, output_grad)
    weights = featurizer.transpose(1, 0, 2)
    turned, feats = gather_features(inputs.transpose(1, 0, 2), weights, ways)
    tokens, channels = output_grad.shape[0], output_grad.shape[2]
    out, own_grad = hyena(
        feats, short_filter, long_filter, decay_rate, skip_gain, output_grad.reshape(tokens, channels))
    grads, input_grad = input_product(own_grad, weights, ways)
    weight_grad = weight_product(turned, grads.reshape(3, turned.shape[1], channels))
    return out.reshape(output_grad.shape), input_grad.transpose(1, 0, 2), weight_grad.transpose(1, 0, 2)


def solution(mesh):
    in_specs = (
        P("tp", None, "fsdp"),
        P("fsdp", None, "tp"),
        P(None, None, "tp"),
        P("tp", None),
        P("tp"),
        P("tp"),
        P(None, "fsdp", "tp"),
    )
    out_specs = (P(None, "fsdp", "tp"), P("tp", None, "fsdp"), P("fsdp", None, "tp"))
    return jax.shard_map(shards, mesh=mesh, in_specs=in_specs, out_specs=out_specs, check_vma=False)
```

```python
import functools

import jax
import jax.numpy as jnp
from jax import lax
from jax.experimental import pallas as pl
from jax.experimental.pallas import tpu as pltpu
from jax.sharding import PartitionSpec as P

F32 = jnp.float32
BF16 = jnp.bfloat16
MESH = pl.DeviceIdType.MESH
VMEM = pl.BlockSpec(memory_space=pltpu.VMEM)
LANES = 128
HALO = 16
HEAD = 8


def hyena_kernel(
    blocks, width, feat, short, long, decay, skip, upstream, out, grad,
    taps, taps_back, toeplitz, ext_p, ext_g, query, key, value, prod, conv_grad, filt_grad, sems, head_sems,
):
    me = lax.axis_index("fsdp")
    rest = lax.axis_index("tp")
    tokens, channels = out.shape
    filters, taps_count = long.shape
    has_prev = me > 0
    has_next = me < blocks - 1
    prev = jnp.maximum(me - 1, 0)
    later = jnp.minimum(me + 1, blocks - 1)
    barrier = pltpu.get_barrier_semaphore()

    for peer in (lax.rem(me + 1, blocks), lax.rem(me + blocks - 1, blocks)):
        pl.semaphore_signal(barrier, inc=1, device_id=(peer, rest), device_id_type=MESH)
    pl.semaphore_wait(barrier, 2)

    def front(at, _):
        cols = pl.ds(pl.multiple_of(at * LANES, LANES), LANES)
        parts = []
        for i in range(3):
            f = feat[i, :, cols].astype(F32)
            acc = short[0, pl.ds(i, 1), cols] * f[HALO:]
            for j in range(1, 3):
                acc = acc + short[j, pl.ds(i, 1), cols] * pltpu.roll(f, j, 0)[HALO:]
            parts.append(acc)
        p = parts[1] * parts[2]
        cg = upstream[:, cols].astype(F32) * parts[0]
        query[:, cols] = parts[0]
        key[:, cols] = parts[1]
        value[:, cols] = parts[2]
        prod[:, cols] = p
        conv_grad[:, cols] = cg
        ext_p[pl.ds(tokens, tokens), cols] = p.astype(BF16)
        ext_g[pl.ds(0, tokens), cols] = cg.astype(BF16)
        return 0

    lax.fori_loop(0, channels // LANES, front, 0)

    to_next = pltpu.make_async_remote_copy(
        src_ref=ext_p.at[pl.ds(tokens, tokens)], dst_ref=ext_p.at[pl.ds(0, tokens)],
        send_sem=sems.at[0], recv_sem=sems.at[1], device_id=(later, rest), device_id_type=MESH)
    to_prev = pltpu.make_async_remote_copy(
        src_ref=ext_g.at[pl.ds(0, tokens)], dst_ref=ext_g.at[pl.ds(tokens, tokens)],
        send_sem=sems.at[2], recv_sem=sems.at[3], device_id=(prev, rest), device_id_type=MESH)

    @pl.when(has_next)
    def _():
        to_next.start()

    @pl.when(has_prev)
    def _():
        to_prev.start()

    @pl.when(jnp.logical_not(has_prev))
    def _():
        ext_p[pl.ds(0, tokens), :] = jnp.zeros((tokens, channels), BF16)

    @pl.when(jnp.logical_not(has_next))
    def _():
        ext_g[pl.ds(tokens, tokens), :] = jnp.zeros((tokens, channels), BF16)

    per_tile = LANES // width
    lane = lax.broadcasted_iota(jnp.int32, (tokens, LANES), 1) // width
    high = lax.broadcasted_iota(jnp.int32, (filters, filters), 0)
    wide = lax.broadcasted_iota(jnp.int32, (filters, filters), 1)
    rates = jnp.sum(jnp.where(high == wide, jnp.broadcast_to(decay[...], (filters, filters)), 0.0), 1, keepdims=True)
    steps = lax.broadcasted_iota(jnp.int32, (filters, taps_count), 1).astype(F32)
    taps[...] = (long[...] * jnp.exp(-rates * steps)).astype(BF16).astype(F32)
    rise = lax.broadcasted_iota(jnp.int32, (taps_count, taps_count), 0)
    fall = lax.broadcasted_iota(jnp.int32, (taps_count, taps_count), 1)
    mirror = jnp.where(rise + fall == taps_count - 1, 1.0, 0.0).astype(BF16)
    taps_back[...] = jnp.dot(taps[...].astype(BF16), mirror, preferred_element_type=F32)

    def build(at, _):
        rows = pl.ds(pl.multiple_of(at * per_tile, per_tile), per_tile)
        for way, source, first in ((0, taps_back, 1 + tokens - taps_count), (1, taps, 0)):
            lines = source[rows, :]
            for g in range(per_tile):
                line = jnp.concatenate([lines[g : g + 1], jnp.zeros((1, 2 * tokens - taps_count), F32)], axis=1)
                spread = jnp.broadcast_to(line, (tokens, 2 * tokens))
                spot = pl.ds(pl.multiple_of((at * per_tile + g) * tokens, tokens), tokens)
                toeplitz[way, spot, :] = pltpu.roll(spread, first, 1, stride=1, stride_axis=0).astype(BF16)
        return 0

    lax.fori_loop(0, channels // LANES, build, 0)

    @pl.when(has_prev)
    def _():
        to_next.wait_recv()

    @pl.when(has_next)
    def _():
        to_prev.wait_recv()

    def mixed(at, way, ext):
        spot = pl.ds(pl.multiple_of(at * per_tile * tokens, tokens), per_tile * tokens)
        parts = jnp.dot(toeplitz[way, spot, :], ext, preferred_element_type=F32)
        acc = parts[:tokens]
        for g in range(1, per_tile):
            acc = jnp.where(lane == g, parts[g * tokens : (g + 1) * tokens], acc)
        return acc

    def back(at, _):
        cols = pl.ds(pl.multiple_of(at * LANES, LANES), LANES)
        gain = skip[:, cols]
        conv = mixed(at, 0, ext_p[:, cols]) + gain * prod[:, cols]
        pg = mixed(at, 1, ext_g[:, cols]) + gain * conv_grad[:, cols]
        out[:, cols] = (query[:, cols] * conv).astype(BF16)
        own = pl.ds(0, tokens)
        filt_grad[0, own, cols] = upstream[:, cols].astype(F32) * conv
        filt_grad[1, own, cols] = pg * value[:, cols]
        filt_grad[2, own, cols] = pg * key[:, cols]
        return 0

    lax.fori_loop(0, channels // LANES, back, 0)

    head = pltpu.make_async_remote_copy(
        src_ref=filt_grad.at[:, pl.ds(0, HEAD)], dst_ref=filt_grad.at[:, pl.ds(tokens, HEAD)],
        send_sem=head_sems.at[0], recv_sem=head_sems.at[1], device_id=(prev, rest), device_id_type=MESH)

    @pl.when(has_prev)
    def _():
        head.start()

    @pl.when(jnp.logical_not(has_next))
    def _():
        filt_grad[:, pl.ds(tokens, HEAD), :] = jnp.zeros((3, HEAD, channels), F32)

    @pl.when(has_next)
    def _():
        head.wait_recv()

    def last(at, _):
        cols = pl.ds(pl.multiple_of(at * LANES, LANES), LANES)
        for i in range(3):
            f = filt_grad[i, :, cols]
            acc = short[0, pl.ds(i, 1), cols] * f[:tokens]
            for j in range(1, 3):
                acc = acc + short[j, pl.ds(i, 1), cols] * pltpu.roll(f, tokens + HEAD - j, 0)[:tokens]
            grad[i, :, cols] = acc.astype(BF16)
        return 0

    lax.fori_loop(0, channels // LANES, last, 0)

    @pl.when(has_next)
    def _():
        to_next.wait_send()

    @pl.when(has_prev)
    def _():
        to_prev.wait_send()
        head.wait_send()


def hyena(feat, short_filter, long_filter, decay_rate, skip_gain, upstream):
    tokens, channels = upstream.shape
    filters, taps_count = long_filter.shape
    width = channels // filters
    wide = pltpu.VMEM((tokens, channels), F32)
    return pl.pallas_call(
        functools.partial(hyena_kernel, lax.axis_size("fsdp"), width),
        out_shape=(jax.ShapeDtypeStruct((tokens, channels), BF16), jax.ShapeDtypeStruct((3, tokens, channels), BF16)),
        in_specs=[VMEM] * 6,
        out_specs=(VMEM, VMEM),
        scratch_shapes=[
            pltpu.VMEM((filters, taps_count), F32), pltpu.VMEM((filters, taps_count), F32),
            pltpu.VMEM((2, filters * tokens, 2 * tokens), BF16),
            pltpu.VMEM((2 * tokens, channels), BF16), pltpu.VMEM((2 * tokens, channels), BF16),
            wide, wide, wide, wide, wide, pltpu.VMEM((3, tokens + HEAD, channels), F32),
            pltpu.SemaphoreType.DMA((4,)), pltpu.SemaphoreType.DMA((2,)),
        ],
        compiler_params=pltpu.CompilerParams(collective_id=1, has_side_effects=True, vmem_limit_bytes=40 * 2**20),
    )(feat, short_filter, long_filter, decay_rate[None], skip_gain[None], upstream)


def remote(src, dst, send, recv, where):
    return pltpu.make_async_remote_copy(
        src_ref=src, dst_ref=dst, send_sem=send, recv_sem=recv, device_id=where, device_id_type=MESH)


class Place:
    def __init__(self, levels):
        self.f = lax.axis_index("fsdp")
        self.t = lax.axis_index("tp")
        self.levels = levels
        self.z, self.y = self.t // 2, lax.rem(self.t, 2)
        self.x, self.core = self.f // 2, lax.rem(self.f, 2)
        self.pair = (self.f, 2 * self.z + 1 - self.y)
        self.up = (self.f, 2 * lax.rem(self.z + 1, levels) + self.y)
        self.down = (self.f, 2 * lax.rem(self.z + levels - 1, levels) + self.y)
        self.twin = (2 * self.x + 1 - self.core, self.t)
        self.across = (2 * (1 - self.x) + self.core, self.t)

    def nearest(self, step):
        levels, z = self.levels, self.z
        paired = jnp.minimum(z, levels - 1 - z)
        near = (step + 1) // 2 * (1 if step % 2 == 0 else -1)
        far = (step - paired) * jnp.where(z < levels - 1 - z, 1, -1)
        return z + jnp.where(step <= 2 * paired, near, far)

    def greet(self):
        barrier = pltpu.get_barrier_semaphore()
        peers = (self.pair, self.up, self.down, self.twin, self.across)
        for peer in peers:
            pl.semaphore_signal(barrier, inc=1, device_id=peer, device_id_type=MESH)
        pl.semaphore_wait(barrier, len(peers))


def features_kernel(
    levels, cuts, x, w, turned, feat,
    gath, wv, result, mine, total, to_twin, from_twin, to_far, from_far,
    w_sem, got, pair_sem, up_sem, down_sem, twin_send, twin_got, far_send, far_got, edge_send, edge_got,
):
    at = Place(levels)
    blocks, own, depth = x.shape
    tokens, channels = gath.shape[1], w.shape[2]
    part = depth // cuts
    both = 2 * own
    loads = [pltpu.make_async_copy(w.at[i], wv.at[i], w_sem.at[i]) for i in range(3)]
    for load in loads:
        load.start()
    gath[:, pl.ds(pl.multiple_of(at.t * own, own), own), :] = x[...]
    at.greet()

    def shard(t, h):
        return gath.at[:, pl.ds(pl.multiple_of(t * own, own), own), pl.ds(h * part, part)]

    def push(t, h, send, where):
        return remote(shard(t, h), shard(t, h), send, got.at[t, h], where)

    def source(k):
        return 2 * (at.z - k) + at.y

    def upward(k, h):
        return push(source(k), h, up_sem.at[k, h], at.up)

    def downward(k, h):
        return push(source(-k), h, down_sem.at[k, h], at.down)

    def sideways(k, h):
        return push(source(k), h, pair_sem.at[k + levels, h], at.pair)

    can_up, can_down = at.z < levels - 1, at.z > 0
    for h in range(cuts):
        @pl.when(can_up)
        def _():
            upward(0, h).start()

        @pl.when(can_down)
        def _():
            downward(0, h).start()

        sideways(0, h).start()

    tile = min(256, channels)
    main, edge = pl.ds(0, both), pl.ds(both, HALO)
    last = levels - 1

    def swap(n, i):
        return remote(to_twin.at[n, i], from_twin.at[n, i], twin_send.at[n, i], twin_got.at[n, i], at.twin)

    def far(i, z):
        spot = pl.ds(pl.multiple_of(HALO + z * both, HALO), both)
        return remote(to_far.at[i, spot], from_far.at[i, spot], far_send.at[i, z], far_got.at[i, z], at.across)

    def far_edge(i):
        spot = pl.ds(0, HALO)
        return remote(to_far.at[i, spot], from_far.at[i, spot], edge_send.at[i], edge_got.at[i], at.across)

    def passed_on(n, i):
        z = at.nearest(n)
        spot = pl.ds(pl.multiple_of(HALO + z * both, HALO), both)
        slot = (3 * n + i) % 2
        swap(n, i).wait_recv()
        to_far[i, spot] = (mine[slot, 0, main] + from_twin[n, i, 0, main].astype(F32)).astype(BF16)
        far(i, z).start()
        total[i, spot] = mine[slot, 1, main] + from_twin[n, i, 1, main].astype(F32)

        @pl.when(z == last)
        def _():
            spot = pl.ds(0, HALO)
            to_far[i, spot] = (mine[slot, 0, edge] + from_twin[n, i, 0, edge].astype(F32)).astype(BF16)
            far_edge(i).start()
            total[i, spot] = mine[slot, 1, edge] + from_twin[n, i, 1, edge].astype(F32)

    def group(n):
        z = at.nearest(n)
        for h in range(cuts):
            push(2 * z + 1 - at.y, h, pair_sem.at[0, 0], at.pair).wait_recv()
        spot = pl.ds(pl.multiple_of(z * both, both), both)
        for i in range(3):
            if n == 0:
                loads[i].wait()

            def step(m, _):
                cols = pl.ds(pl.multiple_of(m * tile, tile), tile)
                lines = gath[:, spot, :].reshape(blocks * both, depth)
                term = jnp.dot(lines, wv[i, :, cols], preferred_element_type=F32)
                result[:, :, cols] = term.reshape(blocks, both, tile)
                return 0

            lax.fori_loop(0, channels // tile, step, 0)
            slot = (3 * n + i) % 2
            for phase in range(2):
                side = 1 - at.x if phase == 0 else at.x
                for other in range(2):
                    block = 2 * side + (1 - at.core if other else at.core)
                    before = result[jnp.maximum(block - 1, 0), pl.ds(both - HALO, HALO), :]
                    before = jnp.where(block > 0, before, jnp.zeros_like(before))
                    if other:
                        to_twin[n, i, phase, main] = result[block].astype(BF16)
                        to_twin[n, i, phase, edge] = before.astype(BF16)
                    else:
                        mine[slot, phase, main] = result[block]
                        mine[slot, phase, edge] = before
            swap(n, i).start()
            if n + i > 0:
                passed_on(n if i > 0 else n - 1, i - 1 if i > 0 else 2)

    for k in range(1, levels):
        for h in range(cuts):
            @pl.when(at.z >= k)
            def _():
                sideways(k, h).wait_recv()

                @pl.when(can_up)
                def _():
                    upward(k, h).start()

                sideways(k, h).start()

            @pl.when(at.z + k < levels)
            def _():
                sideways(-k, h).wait_recv()

                @pl.when(can_down)
                def _():
                    downward(k, h).start()

                sideways(-k, h).start()
        group(k - 1)
    group(levels - 1)
    passed_on(levels - 1, 2)
    for n in range(depth // tile):
        cols = pl.ds(n * tile, tile)
        turned[cols, :] = gath[:, :, cols].reshape(blocks * tokens, tile).T
    for i in range(3):
        for z in range(levels):
            far(i, z).wait_recv()
        far_edge(i).wait_recv()
        feat[i] = (total[i] + from_far[i].astype(F32)).astype(BF16)

    for i in range(3):
        for n in range(levels):
            far(i, n).wait_send()
            swap(n, i).wait_send()
        far_edge(i).wait_send()
    for h in range(cuts):
        for k in range(levels):
            @pl.when(jnp.logical_and(can_up, at.z >= k))
            def _():
                upward(k, h).wait_send()

            @pl.when(jnp.logical_and(can_down, at.z + k < levels))
            def _():
                downward(k, h).wait_send()

            @pl.when(at.z >= k)
            def _():
                sideways(k, h).wait_send()

            if k > 0:
                @pl.when(at.z + k < levels)
                def _():
                    sideways(-k, h).wait_send()


def gather_features(x, w, ways):
    blocks, own, depth = x.shape
    channels = w.shape[2]
    levels, cuts = ways // 2, 2
    tokens = own * ways
    span = tokens + HALO
    half = pltpu.VMEM((3, span, channels), BF16)
    swaps = pltpu.VMEM((levels, 3, 2, 2 * own + HALO, channels), BF16)
    dma = pltpu.SemaphoreType.DMA
    return pl.pallas_call(
        functools.partial(features_kernel, levels, cuts),
        out_shape=(
            jax.ShapeDtypeStruct((depth, blocks * tokens), BF16), jax.ShapeDtypeStruct((3, span, channels), BF16)),
        in_specs=[VMEM, pl.BlockSpec(memory_space=pl.ANY)],
        out_specs=(VMEM, VMEM),
        scratch_shapes=[
            pltpu.VMEM((blocks, tokens, depth), BF16), pltpu.VMEM(w.shape, BF16),
            pltpu.VMEM((blocks, 2 * own, channels), F32), pltpu.VMEM((2, 2, 2 * own + HALO, channels), F32),
            pltpu.VMEM((3, span, channels), F32), swaps, swaps, half, half,
            dma((3,)), dma((ways, cuts)), dma((2 * levels, cuts)), dma((levels, cuts)), dma((levels, cuts)),
            dma((levels, 3)), dma((levels, 3)), dma((3, levels)), dma((3, levels)), dma((3,)), dma((3,)),
        ],
        compiler_params=pltpu.CompilerParams(collective_id=0, has_side_effects=True, vmem_limit_bytes=48 * 2**20),
    )(x, w)


def input_grad_kernel(
    levels, g, w, grads, out,
    wv, partial, side_in, up_in, down_in, staged, total,
    w_sem, twin_send, twin_got, far_send, far_got, pass_send, pass_got,
    side_send, side_got, line_send, up_got, down_got,
):
    at = Place(levels)
    blocks, own, depth = out.shape
    channels, tokens = g.shape[2], g.shape[1]
    loads = [pltpu.make_async_copy(w.at[i], wv.at[i], w_sem.at[i]) for i in range(3)]
    for load in loads:
        load.start()
    for i in range(3):
        grads[i, at.f] = g[i]
    at.greet()
    there = 2 * (1 - at.x) + at.core
    both = 2 * own

    def level(step):
        return at.nearest(levels - 1 - step)

    def strip(block, z):
        return grads.at[:, block, pl.ds(pl.multiple_of(z * both, both), both)]

    def to_far(z):
        return remote(strip(at.f, z), strip(at.f, z), far_send.at[z], far_got.at[z], at.across)

    def to_twin(i):
        return remote(grads.at[i, at.f], grads.at[i, at.f], twin_send.at[i], twin_got.at[i], at.twin)

    def passed(z):
        return remote(strip(there, z), strip(there, z), pass_send.at[z], pass_got.at[z], at.twin)

    for step in range(levels):
        to_far(level(step)).start()
    for i in range(3):
        to_twin(i).start()

    tile = min(256, depth)

    def multiply(half, start, count, first, stop):
        side = at.x if half == 0 else 1 - at.x
        span = pl.ds(start, count)

        def step(n, _):
            cols = pl.ds(pl.multiple_of(n * tile, tile), tile)
            acc = None
            for i in range(3):
                lines = grads[i, pl.ds(2 * side, 2), span].reshape(2 * count, channels)
                term = lax.dot_general(lines, wv[i, cols, :], (((1,), (1,)), ((), ())), preferred_element_type=F32)
                acc = term if acc is None else acc + term
            partial[half, :, span, cols] = acc.astype(BF16).reshape(2, count, tile)
            return 0

        lax.fori_loop(first, stop, step, 0)

    tiles = depth // tile
    cuts = min(4, tiles)
    width = depth // cuts

    def piece(half, t):
        return partial.at[half, :, pl.ds(pl.multiple_of(t * own, own), own)]

    def sideways(half, z, cut):
        cols = pl.ds(cut * width, width)
        return remote(
            piece(half, 2 * z + 1 - at.y).at[:, :, cols], side_in.at[half, z, :, :, cols],
            side_send.at[half, z, cut], side_got.at[half, z, cut], at.pair)

    def upward(half, z):
        return remote(staged.at[half, z], up_in.at[half, z], line_send.at[half, z], up_got.at[half, z], at.up)

    def downward(half, z):
        return remote(staged.at[half, z], down_in.at[half, z], line_send.at[half, z], down_got.at[half, z], at.down)

    def own_sum(half, z):
        for cut in range(cuts):
            sideways(half, z, cut).wait_recv()
        return piece(half, 2 * z + at.y)[...].astype(F32) + side_in[half, z].astype(F32)

    def line(half, z):
        staged[half, z] = own_sum(half, z).astype(BF16)

        @pl.when(z > at.z)
        def _():
            @pl.when(at.z > 0)
            def _():
                upward(half, z).wait_recv()
                staged[half, z] = (staged[half, z].astype(F32) + up_in[half, z].astype(F32)).astype(BF16)

            upward(half, z).start()

        @pl.when(z < at.z)
        def _():
            @pl.when(at.z < levels - 1)
            def _():
                downward(half, z).wait_recv()
                staged[half, z] = (staged[half, z].astype(F32) + down_in[half, z].astype(F32)).astype(BF16)

            downward(half, z).start()

    def finish(half):
        z = at.z
        side = at.x if half == 0 else 1 - at.x
        total[...] = own_sum(half, z)

        @pl.when(z > 0)
        def _():
            upward(half, z).wait_recv()
            total[...] += up_in[half, z].astype(F32)

        @pl.when(z < levels - 1)
        def _():
            downward(half, z).wait_recv()
            total[...] += down_in[half, z].astype(F32)

        out[pl.ds(2 * side, 2)] = total[...].astype(BF16)

    for i in range(3):
        loads[i].wait()
        to_twin(i).wait_recv()
    for cut in range(cuts):
        multiply(0, 0, tokens, cut * tiles // cuts, (cut + 1) * tiles // cuts)
        for step in range(levels):
            sideways(0, level(step), cut).start()
    for step in range(levels):
        z = level(step)
        to_far(z).wait_recv()
        passed(z).start()
        if step < levels - 1:
            line(0, z)
        passed(z).wait_recv()
        for cut in range(cuts):
            multiply(1, pl.multiple_of(z * both, both), both, cut * tiles // cuts, (cut + 1) * tiles // cuts)
            sideways(1, z, cut).start()
        if step > 0:
            line(1, level(step - 1))
    finish(0)
    finish(1)

    for i in range(3):
        to_twin(i).wait_send()
    for z in range(levels):
        to_far(z).wait_send()
        passed(z).wait_send()
        for half in range(2):
            for cut in range(cuts):
                sideways(half, z, cut).wait_send()

            @pl.when(z != at.z)
            def _():
                upward(half, z).wait_send()


def input_product(g, w, ways):
    blocks, tokens, channels = 4, g.shape[1], g.shape[2]
    depth = w.shape[1]
    levels, own = ways // 2, tokens // ways
    pieces = pltpu.VMEM((2, levels, 2, own, depth), BF16)
    dma = pltpu.SemaphoreType.DMA
    lines = dma((2, levels))
    return pl.pallas_call(
        functools.partial(input_grad_kernel, levels),
        out_shape=(
            jax.ShapeDtypeStruct((3, blocks, tokens, channels), BF16),
            jax.ShapeDtypeStruct((blocks, own, depth), BF16)),
        in_specs=[VMEM, pl.BlockSpec(memory_space=pl.ANY)],
        out_specs=(VMEM, VMEM),
        scratch_shapes=[
            pltpu.VMEM(w.shape, BF16), pltpu.VMEM((2, 2, tokens, depth), BF16), pieces, pieces, pieces, pieces,
            pltpu.VMEM((2, own, depth), F32),
            dma((3,)), dma((3,)), dma((3,)), dma((levels,)), dma((levels,)), dma((levels,)), dma((levels,)),
            dma((2, levels, 4)), dma((2, levels, 4)), lines, lines, lines,
        ],
        compiler_params=pltpu.CompilerParams(collective_id=2, has_side_effects=True, vmem_limit_bytes=48 * 2**20),
    )(g, w)


def weight_kernel(x, g, out):
    out[...] = jnp.dot(x[...], g[...], preferred_element_type=F32).astype(BF16)


def weight_product(x, grads):
    depth, rows = x.shape
    channels = grads.shape[2]
    step = min(256, channels)
    return pl.pallas_call(
        weight_kernel,
        grid=(3, channels // step),
        out_shape=jax.ShapeDtypeStruct((3, depth, channels), BF16),
        in_specs=[
            pl.BlockSpec((depth, rows), lambda i, n: (0, 0)),
            pl.BlockSpec((None, rows, step), lambda i, n: (i, 0, n)),
        ],
        out_specs=pl.BlockSpec((None, depth, step), lambda i, n: (i, 0, n)),
        compiler_params=pltpu.CompilerParams(vmem_limit_bytes=40 * 2**20),
        cost_estimate=pl.CostEstimate(
            flops=6 * rows * depth * channels, bytes_accessed=2 * 3 * depth * channels, transcendentals=0),
    )(x, grads)


def shards_general(inputs, featurizer, short_filter, long_filter, decay_rate, skip_gain, output_grad):
    weights = featurizer.transpose(1, 0, 2)
    gathered = lax.all_gather(inputs.transpose(1, 0, 2), "tp", axis=1, tiled=True)
    blocks, tokens, depth = gathered.shape
    channels = weights.shape[2]
    border = jnp.zeros((1, HALO, depth), BF16)
    earlier = jnp.concatenate([border, gathered[: blocks - 1, tokens - HALO :]], axis=0)
    extended = jnp.concatenate([earlier, gathered], axis=1).reshape(blocks * (tokens + HALO), depth)
    feats = []
    for i in range(3):
        part = jnp.dot(extended, weights[i], preferred_element_type=F32).astype(BF16)
        part = part.reshape(blocks, tokens + HALO, channels)
        swapped = lax.all_to_all(part, "fsdp", split_axis=0, concat_axis=0, tiled=True)
        feats.append(jnp.sum(swapped.astype(F32), axis=0).astype(BF16))
    out, own_grad = hyena(
        jnp.stack(feats), short_filter, long_filter, decay_rate, skip_gain, output_grad.reshape(tokens, channels))
    grads = lax.all_gather(own_grad, "fsdp", axis=1, tiled=True)
    turned = grads.reshape(3, blocks, tokens, channels).transpose(0, 2, 1, 3).reshape(grads.shape)
    part = None
    for i in range(3):
        term = lax.dot_general(turned[i], weights[i], (((1,), (1,)), ((), ())), preferred_element_type=F32)
        part = term if part is None else part + term
    weight_grad = weight_product(gathered.reshape(blocks * tokens, depth).T, grads)
    input_grad = lax.psum_scatter(
        part.astype(BF16).reshape(tokens, blocks, depth), "tp", scatter_dimension=0, tiled=True)
    return out.reshape(output_grad.shape), input_grad, weight_grad.transpose(1, 0, 2)


def shards(inputs, featurizer, short_filter, long_filter, decay_rate, skip_gain, output_grad):
    ways = lax.axis_size("tp")
    if inputs.shape[0] % 16 or lax.axis_size("fsdp") != 4 or ways % 4:
        return shards_general(inputs, featurizer, short_filter, long_filter, decay_rate, skip_gain, output_grad)
    weights = featurizer.transpose(1, 0, 2)
    turned, feats = gather_features(inputs.transpose(1, 0, 2), weights, ways)
    tokens, channels = output_grad.shape[0], output_grad.shape[2]
    out, own_grad = hyena(
        feats, short_filter, long_filter, decay_rate, skip_gain, output_grad.reshape(tokens, channels))
    grads, input_grad = input_product(own_grad, weights, ways)
    weight_grad = weight_product(turned, grads.reshape(3, turned.shape[1], channels))
    return out.reshape(output_grad.shape), input_grad.transpose(1, 0, 2), weight_grad.transpose(1, 0, 2)


def solution(mesh):
    in_specs = (
        P("tp", None, "fsdp"),
        P("fsdp", None, "tp"),
        P(None, None, "tp"),
        P("tp", None),
        P("tp"),
        P("tp"),
        P(None, "fsdp", "tp"),
    )
    out_specs = (P(None, "fsdp", "tp"), P("tp", None, "fsdp"), P("fsdp", None, "tp"))
    return jax.shard_map(shards, mesh=mesh, in_specs=in_specs, out_specs=out_specs, check_vma=False)
```

```python
import functools

import jax
import jax.numpy as jnp
from jax import lax
from jax.experimental import pallas as pl
from jax.experimental.pallas import tpu as pltpu
from jax.sharding import PartitionSpec as P

F32 = jnp.float32
BF16 = jnp.bfloat16
MESH = pl.DeviceIdType.MESH
VMEM = pl.BlockSpec(memory_space=pltpu.VMEM)
LANES = 128
HALO = 16
HEAD = 8


def hyena_kernel(
    blocks, width, feat, short, long, decay, skip, upstream, out, grad,
    taps, taps_back, toeplitz, ext_p, ext_g, query, key, value, prod, conv_grad, filt_grad, sems, head_sems,
):
    me = lax.axis_index("fsdp")
    rest = lax.axis_index("tp")
    tokens, channels = out.shape
    filters, taps_count = long.shape
    has_prev = me > 0
    has_next = me < blocks - 1
    prev = jnp.maximum(me - 1, 0)
    later = jnp.minimum(me + 1, blocks - 1)
    barrier = pltpu.get_barrier_semaphore()

    for peer in (lax.rem(me + 1, blocks), lax.rem(me + blocks - 1, blocks)):
        pl.semaphore_signal(barrier, inc=1, device_id=(peer, rest), device_id_type=MESH)
    pl.semaphore_wait(barrier, 2)

    def front(at, _):
        cols = pl.ds(pl.multiple_of(at * LANES, LANES), LANES)
        parts = []
        for i in range(3):
            f = feat[i, :, cols].astype(F32)
            acc = short[0, pl.ds(i, 1), cols] * f[HALO:]
            for j in range(1, 3):
                acc = acc + short[j, pl.ds(i, 1), cols] * pltpu.roll(f, j, 0)[HALO:]
            parts.append(acc)
        p = parts[1] * parts[2]
        cg = upstream[:, cols].astype(F32) * parts[0]
        query[:, cols] = parts[0]
        key[:, cols] = parts[1]
        value[:, cols] = parts[2]
        prod[:, cols] = p
        conv_grad[:, cols] = cg
        ext_p[pl.ds(tokens, tokens), cols] = p.astype(BF16)
        ext_g[pl.ds(0, tokens), cols] = cg.astype(BF16)
        return 0

    lax.fori_loop(0, channels // LANES, front, 0)

    to_next = pltpu.make_async_remote_copy(
        src_ref=ext_p.at[pl.ds(tokens, tokens)], dst_ref=ext_p.at[pl.ds(0, tokens)],
        send_sem=sems.at[0], recv_sem=sems.at[1], device_id=(later, rest), device_id_type=MESH)
    to_prev = pltpu.make_async_remote_copy(
        src_ref=ext_g.at[pl.ds(0, tokens)], dst_ref=ext_g.at[pl.ds(tokens, tokens)],
        send_sem=sems.at[2], recv_sem=sems.at[3], device_id=(prev, rest), device_id_type=MESH)

    @pl.when(has_next)
    def _():
        to_next.start()

    @pl.when(has_prev)
    def _():
        to_prev.start()

    @pl.when(jnp.logical_not(has_prev))
    def _():
        ext_p[pl.ds(0, tokens), :] = jnp.zeros((tokens, channels), BF16)

    @pl.when(jnp.logical_not(has_next))
    def _():
        ext_g[pl.ds(tokens, tokens), :] = jnp.zeros((tokens, channels), BF16)

    per_tile = LANES // width
    lane = lax.broadcasted_iota(jnp.int32, (tokens, LANES), 1) // width
    high = lax.broadcasted_iota(jnp.int32, (filters, filters), 0)
    wide = lax.broadcasted_iota(jnp.int32, (filters, filters), 1)
    rates = jnp.sum(jnp.where(high == wide, jnp.broadcast_to(decay[...], (filters, filters)), 0.0), 1, keepdims=True)
    steps = lax.broadcasted_iota(jnp.int32, (filters, taps_count), 1).astype(F32)
    taps[...] = (long[...] * jnp.exp(-rates * steps)).astype(BF16).astype(F32)
    rise = lax.broadcasted_iota(jnp.int32, (taps_count, taps_count), 0)
    fall = lax.broadcasted_iota(jnp.int32, (taps_count, taps_count), 1)
    mirror = jnp.where(rise + fall == taps_count - 1, 1.0, 0.0).astype(BF16)
    taps_back[...] = jnp.dot(taps[...].astype(BF16), mirror, preferred_element_type=F32)

    def build(at, _):
        rows = pl.ds(pl.multiple_of(at * per_tile, per_tile), per_tile)
        for way, source, first in ((0, taps_back, 1 + tokens - taps_count), (1, taps, 0)):
            lines = source[rows, :]
            for g in range(per_tile):
                line = jnp.concatenate([lines[g : g + 1], jnp.zeros((1, 2 * tokens - taps_count), F32)], axis=1)
                spread = jnp.broadcast_to(line, (tokens, 2 * tokens))
                spot = pl.ds(pl.multiple_of((at * per_tile + g) * tokens, tokens), tokens)
                toeplitz[way, spot, :] = pltpu.roll(spread, first, 1, stride=1, stride_axis=0).astype(BF16)
        return 0

    lax.fori_loop(0, channels // LANES, build, 0)

    @pl.when(has_prev)
    def _():
        to_next.wait_recv()

    @pl.when(has_next)
    def _():
        to_prev.wait_recv()

    def mixed(at, way, ext):
        spot = pl.ds(pl.multiple_of(at * per_tile * tokens, tokens), per_tile * tokens)
        parts = jnp.dot(toeplitz[way, spot, :], ext, preferred_element_type=F32)
        acc = parts[:tokens]
        for g in range(1, per_tile):
            acc = jnp.where(lane == g, parts[g * tokens : (g + 1) * tokens], acc)
        return acc

    def back(at, _):
        cols = pl.ds(pl.multiple_of(at * LANES, LANES), LANES)
        gain = skip[:, cols]
        conv = mixed(at, 0, ext_p[:, cols]) + gain * prod[:, cols]
        pg = mixed(at, 1, ext_g[:, cols]) + gain * conv_grad[:, cols]
        out[:, cols] = (query[:, cols] * conv).astype(BF16)
        own = pl.ds(0, tokens)
        filt_grad[0, own, cols] = upstream[:, cols].astype(F32) * conv
        filt_grad[1, own, cols] = pg * value[:, cols]
        filt_grad[2, own, cols] = pg * key[:, cols]
        return 0

    lax.fori_loop(0, channels // LANES, back, 0)

    head = pltpu.make_async_remote_copy(
        src_ref=filt_grad.at[:, pl.ds(0, HEAD)], dst_ref=filt_grad.at[:, pl.ds(tokens, HEAD)],
        send_sem=head_sems.at[0], recv_sem=head_sems.at[1], device_id=(prev, rest), device_id_type=MESH)

    @pl.when(has_prev)
    def _():
        head.start()

    @pl.when(jnp.logical_not(has_next))
    def _():
        filt_grad[:, pl.ds(tokens, HEAD), :] = jnp.zeros((3, HEAD, channels), F32)

    @pl.when(has_next)
    def _():
        head.wait_recv()

    def last(at, _):
        cols = pl.ds(pl.multiple_of(at * LANES, LANES), LANES)
        for i in range(3):
            f = filt_grad[i, :, cols]
            acc = short[0, pl.ds(i, 1), cols] * f[:tokens]
            for j in range(1, 3):
                acc = acc + short[j, pl.ds(i, 1), cols] * pltpu.roll(f, tokens + HEAD - j, 0)[:tokens]
            grad[i, :, cols] = acc.astype(BF16)
        return 0

    lax.fori_loop(0, channels // LANES, last, 0)

    @pl.when(has_next)
    def _():
        to_next.wait_send()

    @pl.when(has_prev)
    def _():
        to_prev.wait_send()
        head.wait_send()


def hyena(feat, short_filter, long_filter, decay_rate, skip_gain, upstream):
    tokens, channels = upstream.shape
    filters, taps_count = long_filter.shape
    width = channels // filters
    wide = pltpu.VMEM((tokens, channels), F32)
    return pl.pallas_call(
        functools.partial(hyena_kernel, lax.axis_size("fsdp"), width),
        out_shape=(jax.ShapeDtypeStruct((tokens, channels), BF16), jax.ShapeDtypeStruct((3, tokens, channels), BF16)),
        in_specs=[VMEM] * 6,
        out_specs=(VMEM, VMEM),
        scratch_shapes=[
            pltpu.VMEM((filters, taps_count), F32), pltpu.VMEM((filters, taps_count), F32),
            pltpu.VMEM((2, filters * tokens, 2 * tokens), BF16),
            pltpu.VMEM((2 * tokens, channels), BF16), pltpu.VMEM((2 * tokens, channels), BF16),
            wide, wide, wide, wide, wide, pltpu.VMEM((3, tokens + HEAD, channels), F32),
            pltpu.SemaphoreType.DMA((4,)), pltpu.SemaphoreType.DMA((2,)),
        ],
        compiler_params=pltpu.CompilerParams(collective_id=1, has_side_effects=True, vmem_limit_bytes=40 * 2**20),
    )(feat, short_filter, long_filter, decay_rate[None], skip_gain[None], upstream)


def remote(src, dst, send, recv, where):
    return pltpu.make_async_remote_copy(
        src_ref=src, dst_ref=dst, send_sem=send, recv_sem=recv, device_id=where, device_id_type=MESH)


class Place:
    def __init__(self, levels):
        self.f = lax.axis_index("fsdp")
        self.t = lax.axis_index("tp")
        self.levels = levels
        self.z, self.y = self.t // 2, lax.rem(self.t, 2)
        self.x, self.core = self.f // 2, lax.rem(self.f, 2)
        self.pair = (self.f, 2 * self.z + 1 - self.y)
        self.up = (self.f, 2 * lax.rem(self.z + 1, levels) + self.y)
        self.down = (self.f, 2 * lax.rem(self.z + levels - 1, levels) + self.y)
        self.twin = (2 * self.x + 1 - self.core, self.t)
        self.across = (2 * (1 - self.x) + self.core, self.t)

    def nearest(self, step):
        levels, z = self.levels, self.z
        paired = jnp.minimum(z, levels - 1 - z)
        near = (step + 1) // 2 * (1 if step % 2 == 0 else -1)
        far = (step - paired) * jnp.where(z < levels - 1 - z, 1, -1)
        return z + jnp.where(step <= 2 * paired, near, far)

    def farthest(self, step):
        half = self.levels // 2
        low = self.z < half
        if step < half:
            return jnp.where(low, self.levels - 1 - step, step)
        local = jnp.where(low, self.z, self.z - half)
        back = self.levels - 1 - step
        paired = jnp.minimum(local, half - 1 - local)
        near = (back + 1) // 2 * (1 if back % 2 == 0 else -1)
        far = (back - paired) * jnp.where(local < half - 1 - local, 1, -1)
        return self.z + jnp.where(back <= 2 * paired, near, far)

    def greet(self):
        barrier = pltpu.get_barrier_semaphore()
        peers = (self.pair, self.up, self.down, self.twin, self.across)
        for peer in peers:
            pl.semaphore_signal(barrier, inc=1, device_id=peer, device_id_type=MESH)
        pl.semaphore_wait(barrier, len(peers))


def features_kernel(
    levels, cuts, x, w, turned, feat,
    gath, wv, result, mine, total, to_twin, from_twin, to_far, from_far,
    w_sem, got, pair_sem, up_sem, down_sem, twin_send, twin_got, far_send, far_got, edge_send, edge_got,
):
    at = Place(levels)
    blocks, own, depth = x.shape
    tokens, channels = gath.shape[1], w.shape[2]
    part = depth // cuts
    both = 2 * own
    loads = [pltpu.make_async_copy(w.at[i], wv.at[i], w_sem.at[i]) for i in range(3)]
    for load in loads:
        load.start()
    gath[:, pl.ds(pl.multiple_of(at.t * own, own), own), :] = x[...]
    at.greet()

    def shard(t, h):
        return gath.at[:, pl.ds(pl.multiple_of(t * own, own), own), pl.ds(h * part, part)]

    def push(t, h, send, where):
        return remote(shard(t, h), shard(t, h), send, got.at[t, h], where)

    def source(k):
        return 2 * (at.z - k) + at.y

    def upward(k, h):
        return push(source(k), h, up_sem.at[k, h], at.up)

    def downward(k, h):
        return push(source(-k), h, down_sem.at[k, h], at.down)

    def sideways(k, h):
        return push(source(k), h, pair_sem.at[k + levels, h], at.pair)

    can_up, can_down = at.z < levels - 1, at.z > 0
    for h in range(cuts):
        @pl.when(can_up)
        def _():
            upward(0, h).start()

        @pl.when(can_down)
        def _():
            downward(0, h).start()

        sideways(0, h).start()

    tile = min(256, channels)
    main, edge = pl.ds(0, both), pl.ds(both, HALO)
    last = levels - 1

    def swap(n, i):
        return remote(to_twin.at[n, i], from_twin.at[n, i], twin_send.at[n, i], twin_got.at[n, i], at.twin)

    def far(i, z):
        spot = pl.ds(pl.multiple_of(HALO + z * both, HALO), both)
        return remote(to_far.at[i, spot], from_far.at[i, spot], far_send.at[i, z], far_got.at[i, z], at.across)

    def far_edge(i):
        spot = pl.ds(0, HALO)
        return remote(to_far.at[i, spot], from_far.at[i, spot], edge_send.at[i], edge_got.at[i], at.across)

    def passed_on(n, i):
        z = at.nearest(n)
        spot = pl.ds(pl.multiple_of(HALO + z * both, HALO), both)
        slot = (3 * n + i) % 2
        swap(n, i).wait_recv()
        to_far[i, spot] = (mine[slot, 0, main] + from_twin[n, i, 0, main].astype(F32)).astype(BF16)
        far(i, z).start()
        total[i, spot] = mine[slot, 1, main] + from_twin[n, i, 1, main].astype(F32)

        @pl.when(z == last)
        def _():
            spot = pl.ds(0, HALO)
            to_far[i, spot] = (mine[slot, 0, edge] + from_twin[n, i, 0, edge].astype(F32)).astype(BF16)
            far_edge(i).start()
            total[i, spot] = mine[slot, 1, edge] + from_twin[n, i, 1, edge].astype(F32)

    def group(n):
        z = at.nearest(n)
        for h in range(cuts):
            push(2 * z + 1 - at.y, h, pair_sem.at[0, 0], at.pair).wait_recv()
        spot = pl.ds(pl.multiple_of(z * both, both), both)
        for i in range(3):
            if n == 0:
                loads[i].wait()

            def step(m, _):
                cols = pl.ds(pl.multiple_of(m * tile, tile), tile)
                lines = gath[:, spot, :].reshape(blocks * both, depth)
                term = jnp.dot(lines, wv[i, :, cols], preferred_element_type=F32)
                result[:, :, cols] = term.reshape(blocks, both, tile)
                return 0

            lax.fori_loop(0, channels // tile, step, 0)
            slot = (3 * n + i) % 2
            for phase in range(2):
                side = 1 - at.x if phase == 0 else at.x
                for other in range(2):
                    block = 2 * side + (1 - at.core if other else at.core)
                    before = result[jnp.maximum(block - 1, 0), pl.ds(both - HALO, HALO), :]
                    before = jnp.where(block > 0, before, jnp.zeros_like(before))
                    if other:
                        to_twin[n, i, phase, main] = result[block].astype(BF16)
                        to_twin[n, i, phase, edge] = before.astype(BF16)
                    else:
                        mine[slot, phase, main] = result[block]
                        mine[slot, phase, edge] = before
            swap(n, i).start()
            if n + i > 0:
                passed_on(n if i > 0 else n - 1, i - 1 if i > 0 else 2)

    for k in range(1, levels):
        for h in range(cuts):
            @pl.when(at.z >= k)
            def _():
                sideways(k, h).wait_recv()

                @pl.when(can_up)
                def _():
                    upward(k, h).start()

                sideways(k, h).start()

            @pl.when(at.z + k < levels)
            def _():
                sideways(-k, h).wait_recv()

                @pl.when(can_down)
                def _():
                    downward(k, h).start()

                sideways(-k, h).start()
        group(k - 1)
    group(levels - 1)
    passed_on(levels - 1, 2)
    for n in range(depth // tile):
        cols = pl.ds(n * tile, tile)
        turned[cols, :] = gath[:, :, cols].reshape(blocks * tokens, tile).T
    for i in range(3):
        for z in range(levels):
            far(i, z).wait_recv()
        far_edge(i).wait_recv()
        feat[i] = (total[i] + from_far[i].astype(F32)).astype(BF16)

    for i in range(3):
        for n in range(levels):
            far(i, n).wait_send()
            swap(n, i).wait_send()
        far_edge(i).wait_send()
    for h in range(cuts):
        for k in range(levels):
            @pl.when(jnp.logical_and(can_up, at.z >= k))
            def _():
                upward(k, h).wait_send()

            @pl.when(jnp.logical_and(can_down, at.z + k < levels))
            def _():
                downward(k, h).wait_send()

            @pl.when(at.z >= k)
            def _():
                sideways(k, h).wait_send()

            if k > 0:
                @pl.when(at.z + k < levels)
                def _():
                    sideways(-k, h).wait_send()


def gather_features(x, w, ways):
    blocks, own, depth = x.shape
    channels = w.shape[2]
    levels, cuts = ways // 2, 2
    tokens = own * ways
    span = tokens + HALO
    half = pltpu.VMEM((3, span, channels), BF16)
    swaps = pltpu.VMEM((levels, 3, 2, 2 * own + HALO, channels), BF16)
    dma = pltpu.SemaphoreType.DMA
    return pl.pallas_call(
        functools.partial(features_kernel, levels, cuts),
        out_shape=(
            jax.ShapeDtypeStruct((depth, blocks * tokens), BF16), jax.ShapeDtypeStruct((3, span, channels), BF16)),
        in_specs=[VMEM, pl.BlockSpec(memory_space=pl.ANY)],
        out_specs=(VMEM, VMEM),
        scratch_shapes=[
            pltpu.VMEM((blocks, tokens, depth), BF16), pltpu.VMEM(w.shape, BF16),
            pltpu.VMEM((blocks, 2 * own, channels), F32), pltpu.VMEM((2, 2, 2 * own + HALO, channels), F32),
            pltpu.VMEM((3, span, channels), F32), swaps, swaps, half, half,
            dma((3,)), dma((ways, cuts)), dma((2 * levels, cuts)), dma((levels, cuts)), dma((levels, cuts)),
            dma((levels, 3)), dma((levels, 3)), dma((3, levels)), dma((3, levels)), dma((3,)), dma((3,)),
        ],
        compiler_params=pltpu.CompilerParams(collective_id=0, has_side_effects=True, vmem_limit_bytes=48 * 2**20),
    )(x, w)


def input_grad_kernel(
    levels, g, w, grads, out,
    wv, partial, side_in, up_in, down_in, staged, total,
    w_sem, twin_send, twin_got, far_send, far_got, pass_send, pass_got,
    side_send, side_got, line_send, up_got, down_got,
):
    at = Place(levels)
    blocks, own, depth = out.shape
    channels, tokens = g.shape[2], g.shape[1]
    loads = [pltpu.make_async_copy(w.at[i], wv.at[i], w_sem.at[i]) for i in range(3)]
    for load in loads:
        load.start()
    for i in range(3):
        grads[i, at.f] = g[i]
    at.greet()
    there = 2 * (1 - at.x) + at.core
    both = 2 * own

    def level(step):
        return at.farthest(step)

    def strip(block, z):
        return grads.at[:, block, pl.ds(pl.multiple_of(z * both, both), both)]

    def to_far(z):
        return remote(strip(at.f, z), strip(at.f, z), far_send.at[z], far_got.at[z], at.across)

    def to_twin(i):
        return remote(grads.at[i, at.f], grads.at[i, at.f], twin_send.at[i], twin_got.at[i], at.twin)

    def passed(z):
        return remote(strip(there, z), strip(there, z), pass_send.at[z], pass_got.at[z], at.twin)

    for step in range(levels):
        to_far(level(step)).start()
    for i in range(3):
        to_twin(i).start()

    tile = min(256, depth)

    def multiply(half, start, count, first, stop):
        side = at.x if half == 0 else 1 - at.x
        span = pl.ds(start, count)

        def step(n, _):
            cols = pl.ds(pl.multiple_of(n * tile, tile), tile)
            acc = None
            for i in range(3):
                lines = grads[i, pl.ds(2 * side, 2), span].reshape(2 * count, channels)
                term = lax.dot_general(lines, wv[i, cols, :], (((1,), (1,)), ((), ())), preferred_element_type=F32)
                acc = term if acc is None else acc + term
            partial[half, :, span, cols] = acc.astype(BF16).reshape(2, count, tile)
            return 0

        lax.fori_loop(first, stop, step, 0)

    tiles = depth // tile
    cuts = 1
    width = depth // cuts

    def piece(half, t):
        return partial.at[half, :, pl.ds(pl.multiple_of(t * own, own), own)]

    def sideways(half, z, cut):
        cols = pl.ds(cut * width, width)
        return remote(
            piece(half, 2 * z + 1 - at.y).at[:, :, cols], side_in.at[half, z, :, :, cols],
            side_send.at[half, z, cut], side_got.at[half, z, cut], at.pair)

    def upward(half, z):
        return remote(staged.at[half, z], up_in.at[half, z], line_send.at[half, z], up_got.at[half, z], at.up)

    def downward(half, z):
        return remote(staged.at[half, z], down_in.at[half, z], line_send.at[half, z], down_got.at[half, z], at.down)

    def own_sum(half, z):
        for cut in range(cuts):
            sideways(half, z, cut).wait_recv()
        return piece(half, 2 * z + at.y)[...].astype(F32) + side_in[half, z].astype(F32)

    def line(half, z):
        staged[half, z] = own_sum(half, z).astype(BF16)

        @pl.when(z > at.z)
        def _():
            @pl.when(at.z > 0)
            def _():
                upward(half, z).wait_recv()
                staged[half, z] = (staged[half, z].astype(F32) + up_in[half, z].astype(F32)).astype(BF16)

            upward(half, z).start()

        @pl.when(z < at.z)
        def _():
            @pl.when(at.z < levels - 1)
            def _():
                downward(half, z).wait_recv()
                staged[half, z] = (staged[half, z].astype(F32) + down_in[half, z].astype(F32)).astype(BF16)

            downward(half, z).start()

    def finish(half):
        z = at.z
        side = at.x if half == 0 else 1 - at.x
        total[...] = own_sum(half, z)

        @pl.when(z > 0)
        def _():
            upward(half, z).wait_recv()
            total[...] += up_in[half, z].astype(F32)

        @pl.when(z < levels - 1)
        def _():
            downward(half, z).wait_recv()
            total[...] += down_in[half, z].astype(F32)

        out[pl.ds(2 * side, 2)] = total[...].astype(BF16)

    for i in range(3):
        loads[i].wait()
        to_twin(i).wait_recv()
    for cut in range(cuts):
        multiply(0, 0, tokens, cut * tiles // cuts, (cut + 1) * tiles // cuts)
        for step in range(levels):
            sideways(0, level(step), cut).start()
    group = levels // 2
    other = jnp.where(at.z < group, group, 0)
    for turn in range(2):
        first = other if turn == 0 else group - other
        for step in range(turn * group, (turn + 1) * group):
            z = level(step)
            to_far(z).wait_recv()
            passed(z).start()
            if step < levels - 1:
                line(0, z)
        for step in range(turn * group, (turn + 1) * group):
            passed(level(step)).wait_recv()
        multiply(1, pl.multiple_of(first * both, both), group * both, 0, tiles)
        for step in range(turn * group, (turn + 1) * group):
            sideways(1, level(step), 0).start()
    for step in range(levels - 1):
        line(1, level(step))
    finish(0)
    finish(1)

    for i in range(3):
        to_twin(i).wait_send()
    for z in range(levels):
        to_far(z).wait_send()
        passed(z).wait_send()
        for half in range(2):
            for cut in range(cuts):
                sideways(half, z, cut).wait_send()

            @pl.when(z != at.z)
            def _():
                upward(half, z).wait_send()


def input_product(g, w, ways):
    blocks, tokens, channels = 4, g.shape[1], g.shape[2]
    depth = w.shape[1]
    levels, own = ways // 2, tokens // ways
    pieces = pltpu.VMEM((2, levels, 2, own, depth), BF16)
    dma = pltpu.SemaphoreType.DMA
    lines = dma((2, levels))
    return pl.pallas_call(
        functools.partial(input_grad_kernel, levels),
        out_shape=(
            jax.ShapeDtypeStruct((3, blocks, tokens, channels), BF16),
            jax.ShapeDtypeStruct((blocks, own, depth), BF16)),
        in_specs=[VMEM, pl.BlockSpec(memory_space=pl.ANY)],
        out_specs=(VMEM, VMEM),
        scratch_shapes=[
            pltpu.VMEM(w.shape, BF16), pltpu.VMEM((2, 2, tokens, depth), BF16), pieces, pieces, pieces, pieces,
            pltpu.VMEM((2, own, depth), F32),
            dma((3,)), dma((3,)), dma((3,)), dma((levels,)), dma((levels,)), dma((levels,)), dma((levels,)),
            dma((2, levels, 1)), dma((2, levels, 1)), lines, lines, lines,
        ],
        compiler_params=pltpu.CompilerParams(collective_id=2, has_side_effects=True, vmem_limit_bytes=48 * 2**20),
    )(g, w)


def weight_kernel(x, g, out):
    out[...] = jnp.dot(x[...], g[...], preferred_element_type=F32).astype(BF16)


def weight_product(x, grads):
    depth, rows = x.shape
    channels = grads.shape[2]
    step = min(256, channels)
    return pl.pallas_call(
        weight_kernel,
        grid=(3, channels // step),
        out_shape=jax.ShapeDtypeStruct((3, depth, channels), BF16),
        in_specs=[
            pl.BlockSpec((depth, rows), lambda i, n: (0, 0)),
            pl.BlockSpec((None, rows, step), lambda i, n: (i, 0, n)),
        ],
        out_specs=pl.BlockSpec((None, depth, step), lambda i, n: (i, 0, n)),
        compiler_params=pltpu.CompilerParams(vmem_limit_bytes=40 * 2**20),
        cost_estimate=pl.CostEstimate(
            flops=6 * rows * depth * channels, bytes_accessed=2 * 3 * depth * channels, transcendentals=0),
    )(x, grads)


def shards_general(inputs, featurizer, short_filter, long_filter, decay_rate, skip_gain, output_grad):
    weights = featurizer.transpose(1, 0, 2)
    gathered = lax.all_gather(inputs.transpose(1, 0, 2), "tp", axis=1, tiled=True)
    blocks, tokens, depth = gathered.shape
    channels = weights.shape[2]
    border = jnp.zeros((1, HALO, depth), BF16)
    earlier = jnp.concatenate([border, gathered[: blocks - 1, tokens - HALO :]], axis=0)
    extended = jnp.concatenate([earlier, gathered], axis=1).reshape(blocks * (tokens + HALO), depth)
    feats = []
    for i in range(3):
        part = jnp.dot(extended, weights[i], preferred_element_type=F32).astype(BF16)
        part = part.reshape(blocks, tokens + HALO, channels)
        swapped = lax.all_to_all(part, "fsdp", split_axis=0, concat_axis=0, tiled=True)
        feats.append(jnp.sum(swapped.astype(F32), axis=0).astype(BF16))
    out, own_grad = hyena(
        jnp.stack(feats), short_filter, long_filter, decay_rate, skip_gain, output_grad.reshape(tokens, channels))
    grads = lax.all_gather(own_grad, "fsdp", axis=1, tiled=True)
    turned = grads.reshape(3, blocks, tokens, channels).transpose(0, 2, 1, 3).reshape(grads.shape)
    part = None
    for i in range(3):
        term = lax.dot_general(turned[i], weights[i], (((1,), (1,)), ((), ())), preferred_element_type=F32)
        part = term if part is None else part + term
    weight_grad = weight_product(gathered.reshape(blocks * tokens, depth).T, grads)
    input_grad = lax.psum_scatter(
        part.astype(BF16).reshape(tokens, blocks, depth), "tp", scatter_dimension=0, tiled=True)
    return out.reshape(output_grad.shape), input_grad, weight_grad.transpose(1, 0, 2)


def shards(inputs, featurizer, short_filter, long_filter, decay_rate, skip_gain, output_grad):
    ways = lax.axis_size("tp")
    if inputs.shape[0] % 16 or lax.axis_size("fsdp") != 4 or ways % 4:
        return shards_general(inputs, featurizer, short_filter, long_filter, decay_rate, skip_gain, output_grad)
    weights = featurizer.transpose(1, 0, 2)
    turned, feats = gather_features(inputs.transpose(1, 0, 2), weights, ways)
    tokens, channels = output_grad.shape[0], output_grad.shape[2]
    out, own_grad = hyena(
        feats, short_filter, long_filter, decay_rate, skip_gain, output_grad.reshape(tokens, channels))
    grads, input_grad = input_product(own_grad, weights, ways)
    weight_grad = weight_product(turned, grads.reshape(3, turned.shape[1], channels))
    return out.reshape(output_grad.shape), input_grad.transpose(1, 0, 2), weight_grad.transpose(1, 0, 2)


def solution(mesh):
    in_specs = (
        P("tp", None, "fsdp"),
        P("fsdp", None, "tp"),
        P(None, None, "tp"),
        P("tp", None),
        P("tp"),
        P("tp"),
        P(None, "fsdp", "tp"),
    )
    out_specs = (P(None, "fsdp", "tp"), P("tp", None, "fsdp"), P("fsdp", None, "tp"))
    return jax.shard_map(shards, mesh=mesh, in_specs=in_specs, out_specs=out_specs, check_vma=False)
```
